32 devices in a mesh: groups: 2 (over y), outer: 4 (over x, core), inner: 4 (over z).
Axes of the slice: x: 2, y: 2, z: 4, core: 2. Of those that a mesh axis runs over, the one named last changes fastest.
Arguments:
- activations: bfloat16 [4096, 8192], P(('groups', 'outer', 'inner')), parts along dimension 0, may hold values from -64 to 64
- upstream: bfloat16 [4096, 768], P(('groups', 'outer', 'inner')), parts along dimension 0, may hold values from -8 to 8
- frozen_weight_matrix: bfloat16 [8192, 768], P(('outer', 'inner')), may hold values from -0.21875 to 0.21875
- master: float32 [1146880], P(('groups', 'outer', 'inner')), parts along dimension 0, may hold values from -6 to 6
- moment: float32 [1146880], P(('groups', 'outer', 'inner')), parts along dimension 0, may hold values from -3 to 3
- second_moment: float32 [1146880], P(('groups', 'outer', 'inner')), parts along dimension 0, may hold values from 0.01 to 1
Outputs:
- input_gradient_rows: bfloat16 [4096, 8192], P(('groups', 'outer', 'inner')), parts along dimension 0
- new_master: float32 [1146880], P(('groups', 'outer', 'inner')), parts along dimension 0
- new_moment: float32 [1146880], P(('groups', 'outer', 'inner')), parts along dimension 0
- new_second: float32 [1146880], P(('groups', 'outer', 'inner')), parts along dimension 0
The draws below stay inside these ranges and needn't reach their ends.
There are 2 independent parts, one for each index of `groups`. The reference program is written for one: setup_inputs(seed, part) draws one part's arguments, and reference() takes and returns one part's arrays. A program takes and returns all parts, laid end to end along the dimension named above; an argument that names none is the same for every part. Nothing has to cross between parts.
All inputs are finite; a program needn't handle non-finite values.
Results may differ from the reference program's by a relative error of at most 0.001.
The reference program's roundings to bfloat16 on the way count: a program that leaves them out, or rounds other values in their place, can miss the bound.
Values may be sent and summed in bfloat16 or wider, within the bound.
A program may use at most 128 MiB of HBM per device.

```python
import math
import jax
import jax.numpy as jnp

D = 8192
VALUE_CHANNELS = 768
ADAPTER_RANK = 64
TOKENS = 2048
PARAMS = 573440


def draw_activations(key, part):
    keys = jax.random.split(jax.random.fold_in(key, 11), 5)
    column_scale = jnp.exp(jnp.log(10.0) * jax.random.uniform(keys[1], (D,), jnp.float32))
    row_scale = jnp.exp(jnp.log(10.0) * jax.random.uniform(keys[2], (TOKENS, 1), jnp.float32))
    offset = jax.random.normal(keys[4], (D,), jnp.float32)
    values = jax.random.normal(keys[0], (TOKENS, D), jnp.float32) + 0.2 * offset
    return jnp.clip(0.1 * values * row_scale * column_scale, -64.0, 64.0).astype(jnp.bfloat16)


def draw_upstream(key, part):
    keys = jax.random.split(jax.random.fold_in(key, 23), 2)
    offset = jax.random.normal(keys[1], (VALUE_CHANNELS,), jnp.float32)
    values = jax.random.normal(keys[0], (TOKENS, VALUE_CHANNELS), jnp.float32) + 0.2 * offset
    return jnp.clip(values, -8.0, 8.0).astype(jnp.bfloat16)


def block_scale(rng, shape, shards, smallest, high):
    def one(axis_at, parts):
        draws = jax.random.uniform(jax.random.fold_in(jax.random.fold_in(rng, 6), axis_at), (parts,), jnp.float32, smallest / len(shards), high / len(shards))
        return jnp.repeat(jnp.exp(draws), shape[axis_at] // parts).reshape((-1,) + (1,) * (len(shape) - axis_at - 1))

    factor_of = one(*shards[0])
    for cut in shards[1:]:
        factor_of = factor_of * one(*cut)
    return factor_of


def gaussian(stream_key, dims, width, most, cuts=(), dtype=jnp.bfloat16):
    result = jax.random.normal(stream_key, dims, jnp.float32) * width
    if len(cuts) > 0:
        result = block_scale(stream_key, dims, cuts, -0.22, 0.18) * result
    return jnp.clip(result, min=-most, max=most).astype(dtype)


def setup_inputs(seed: int = 0, part: int = 0) -> dict:
    seeds = jax.random.split(jax.random.key(seed), 7)
    part_splits = jax.random.split(jax.random.fold_in(seeds[6], part), 7)
    activations = draw_activations(jax.random.fold_in(jax.random.fold_in(seeds[6], part), 71), part)
    upstream = draw_upstream(jax.random.fold_in(jax.random.fold_in(seeds[6], part), 71), part)
    frozen_weight_matrix = gaussian(seeds[2], (D, VALUE_CHANNELS), VALUE_CHANNELS ** -0.5, 0.21875, ((0, 16),))
    master = gaussian(part_splits[3], (PARAMS,), 1.0, 6.0, ((0, 16),), jnp.float32)
    moment = gaussian(part_splits[4], (PARAMS,), 0.3, 3.0, ((0, 16),), jnp.float32)
    second_moment = jnp.clip(jnp.exp(math.log(1.0) - 4.6051702 * jax.random.uniform(part_splits[5], (PARAMS,), jnp.float32) ** block_scale(part_splits[5], (PARAMS,), ((0, 16),), -0.2, 0.2)), 0.01, 1.0)
    return dict(activations=activations, upstream=upstream, frozen_weight_matrix=frozen_weight_matrix, master=master, moment=moment, second_moment=second_moment)


def reference(activations, upstream, frozen_weight_matrix, master, moment, second_moment):
    adapter_scale_factor = 0.5 / math.sqrt(ADAPTER_RANK * VALUE_CHANNELS)
    working = master.astype(jnp.bfloat16)
    down_weight_transposed = working[:ADAPTER_RANK * D].reshape(ADAPTER_RANK, D)
    up_m = working[ADAPTER_RANK * D:].reshape(ADAPTER_RANK, VALUE_CHANNELS)
    rank_gradient = jnp.dot(upstream, up_m.T, preferred_element_type=jnp.float32).astype(jnp.bfloat16)
    input_gradient_rows = (jnp.dot(upstream, frozen_weight_matrix.T, preferred_element_type=jnp.float32) + adapter_scale_factor * jnp.dot(rank_gradient, down_weight_transposed, preferred_element_type=jnp.float32)).astype(jnp.bfloat16)
    projected_rows = jnp.dot(activations, down_weight_transposed.T, preferred_element_type=jnp.float32).astype(jnp.bfloat16)
    down_weight_gradient = adapter_scale_factor * jnp.dot(rank_gradient.T, activations, preferred_element_type=jnp.float32)
    up_weight_gradient = adapter_scale_factor * jnp.dot(projected_rows.T, upstream, preferred_element_type=jnp.float32)
    flat_grad = jnp.concatenate([down_weight_gradient.reshape(-1), up_weight_gradient.reshape(-1)])
    norm = jnp.sqrt(jnp.sum(flat_grad * flat_grad) + 1e-06)
    clipped = flat_grad * jnp.minimum(1.0, math.sqrt(PARAMS) / norm)
    new_moment = 0.9 * moment + 0.1 * clipped
    new_second = 0.999 * second_moment + 0.001 * clipped * clipped
    corr_one = 1.0 - 0.9 ** 10
    corr_two = 1.0 - 0.999 ** 10
    new_master = master - 0.1 * (new_moment / corr_one) / (jnp.sqrt(new_second / corr_two) + 1e-08)
    return (input_gradient_rows, new_master, new_moment, new_second)
```

```python
import functools
import math

import jax
import jax.numpy as jnp
from jax import lax
from jax.experimental import pallas as pl
from jax.experimental.pallas import tpu as pltpu
from jax.sharding import PartitionSpec as P

MESH = pl.DeviceIdType.MESH
LANES = 128
CHUNK = 1024


def per_device(activations, upstream, frozen_weight_matrix, master, moment, second_moment):
    width = activations.shape[1]
    value_width = upstream.shape[1]
    whole = lax.all_gather(master.astype(jnp.bfloat16), ("outer", "inner"), axis=0, tiled=True)
    rank_activations = whole.shape[0] // (width + value_width)
    adapter_scale_factor = 0.5 / math.sqrt(rank_activations * value_width)
    down_weight_transposed = whole[: rank_activations * width].reshape(rank_activations, width)
    up_m = whole[rank_activations * width :].reshape(rank_activations, value_width)
    rank_gradient = jnp.dot(upstream, up_m.T, preferred_element_type=jnp.float32).astype(
        jnp.bfloat16
    )
    projected_rows = jnp.dot(
        activations, down_weight_transposed.T, preferred_element_type=jnp.float32
    ).astype(jnp.bfloat16)
    down_weight_gradient = adapter_scale_factor * jnp.dot(
        rank_gradient.T, activations, preferred_element_type=jnp.float32
    )
    up_weight_gradient = adapter_scale_factor * jnp.dot(
        projected_rows.T, upstream, preferred_element_type=jnp.float32
    )
    flat_grad = jnp.concatenate([down_weight_gradient.reshape(-1), up_weight_gradient.reshape(-1)])
    grad_shard = lax.psum_scatter(flat_grad, ("outer", "inner"), scatter_dimension=0, tiled=True)
    sum_squares = lax.psum(jnp.sum(grad_shard * grad_shard), ("outer", "inner"))
    feat_rows = frozen_weight_matrix.shape[0]
    feat_start = lax.axis_index(("outer", "inner")) * feat_rows
    own_cols = lax.dynamic_slice_in_dim(down_weight_transposed, feat_start, feat_rows, 1)
    tok_piece = lax.all_gather(upstream, ("outer", "inner"), axis=0, tiled=True)
    rank_piece = jnp.dot(tok_piece, up_m.T, preferred_element_type=jnp.float32).astype(jnp.bfloat16)
    frozen_output = lax.dot_general(
        tok_piece,
        frozen_weight_matrix,
        (((1,), (1,)), ((), ())),
        preferred_element_type=jnp.float32,
    )
    feat_block = (
        frozen_output
        + adapter_scale_factor * jnp.dot(rank_piece, own_cols, preferred_element_type=jnp.float32)
    ).astype(jnp.bfloat16)
    n_outer = lax.axis_size("outer")
    n_inner = lax.axis_size("inner")
    tok_count = upstream.shape[0]
    reordered = (
        feat_block.reshape(n_outer, n_inner, tok_count, feat_rows)
        .transpose(1, 0, 2, 3)
        .reshape(n_inner * n_outer * tok_count, feat_rows)
    )
    input_gradient_rows = lax.all_to_all(
        lax.all_to_all(reordered, "inner", split_axis=0, concat_axis=1, tiled=True),
        "outer",
        split_axis=0,
        concat_axis=1,
        tiled=True,
    )
    new_master, new_moment, new_second = adam(
        grad_shard, sum_squares, master, moment, second_moment, whole.shape[0]
    )
    return (input_gradient_rows, new_master, new_moment, new_second)


def adam(grad_shard, sum_squares, master, moment, second_moment, params):
    norm = jnp.sqrt(sum_squares + 1e-06)
    clipped = grad_shard * jnp.minimum(1.0, math.sqrt(params) / norm)
    new_moment = 0.9 * moment + 0.1 * clipped
    new_second = 0.999 * second_moment + 0.001 * clipped * clipped
    corr_one = 1.0 - 0.9**10
    corr_two = 1.0 - 0.999**10
    new_master = master - 0.1 * (new_moment / corr_one) / (jnp.sqrt(new_second / corr_two) + 1e-08)
    return new_master, new_moment, new_second


def dot(a, b, contract):
    return lax.dot_general(
        a, b, (((contract[0],), (contract[1],)), ((), ())), preferred_element_type=jnp.float32
    )


def kernel(
    rank,
    act_ref,
    up_ref,
    w_ref,
    master_ref,
    moment_ref,
    second_ref,
    out_ref,
    new_master_ref,
    new_moment_ref,
    new_second_ref,
    slots,
    flat,
    down,
    up_all,
    w_buf,
    grad,
    from_core,
    half_sum,
    from_x,
    from_z,
    sq_own,
    sq_z,
    sq_line,
    sq_s,
    blocks,
    send_sem,
    recv_sem,
):
    y = lax.axis_index("groups")
    o = lax.axis_index("outer")
    z = lax.axis_index("inner")
    x, c = o // 2, lax.rem(o, 2)
    o_core = 2 * x + (1 - c)
    o_x = 2 * (1 - x) + c
    o_diag = 2 * (1 - x) + (1 - c)
    core_dev, x_dev, diag_dev = {"outer": o_core}, {"outer": o_x}, {"outer": o_diag}
    y_dev = {"groups": 1 - y}
    z_to = [None] + [lax.rem(z + k, 4) for k in range(1, 4)]
    z_from = [z] + [lax.rem(z + 4 - k, 4) for k in range(1, 4)]
    z_devs = [None] + [{"inner": z_to[k]} for k in range(1, 4)]

    tokens, width = act_ref.shape
    value_width = up_ref.shape[1]
    feats = w_ref.shape[0]
    half = feats // 2
    shard_rows = master_ref.shape[0]
    down_rows = rank * width // LANES
    params = 16 * shard_rows * LANES
    scale = 0.5 / math.sqrt(rank * value_width)

    used = []

    def send(src, dst, device):
        at = len(used)
        copy = pltpu.make_async_remote_copy(
            src_ref=src,
            dst_ref=dst,
            send_sem=send_sem.at[at],
            recv_sem=recv_sem.at[at],
            device_id=device,
            device_id_type=MESH,
        )
        used.append(copy)
        copy.start()
        return copy

    own = o * 4 + z
    pad = slots.shape[1] - shard_rows
    slots[own] = jnp.concatenate(
        [master_ref[...], jnp.zeros((pad, LANES), jnp.float32)], axis=0
    ).astype(jnp.bfloat16)
    up_all[o] = up_ref[...]

    barrier = pltpu.get_barrier_semaphore()
    partners = [core_dev, x_dev, diag_dev, y_dev] + z_devs[1:]
    for device in partners:
        pl.semaphore_signal(barrier, inc=1, device_id=device, device_id_type=MESH)
    pl.semaphore_wait(barrier, len(partners))

    slot_z = [None] + [send(slots.at[own], slots.at[own], z_devs[k]) for k in range(1, 4)]
    slot_x = [send(slots.at[own], slots.at[own], x_dev)]
    slot_core = [send(slots.at[own], slots.at[own], core_dev)]
    u_x = send(up_all.at[o], up_all.at[o], x_dev)
    u_core = send(up_all.at[o], up_all.at[o], core_dev)
    my_half = pl.ds(pl.multiple_of(y * half, half), half)
    w_z = [None] + [
        send(w_ref.at[my_half], w_buf.at[k - 1, my_half], z_devs[k]) for k in range(1, 4)
    ]
    for k in range(1, 4):
        slot_z[k].wait_recv()
        at = slots.at[o * 4 + z_from[k]]
        slot_x.append(send(at, at, x_dev))
        slot_core.append(send(at, at, core_dev))
    for k in range(4):
        slot_x[k].wait_recv()
        at = slots.at[o_x * 4 + z_from[k]]
        slot_core.append(send(at, at, core_dev))
    u_x.wait_recv()
    u_far = send(up_all.at[o_x], up_all.at[o_x], core_dev)
    w_y = [None]

    def pass_weight(k):
        w_z[k].wait_recv()
        at = w_buf.at[k - 1, my_half]
        w_y.append(send(at, at, y_dev))

    for copy in slot_core:
        copy.wait_recv()
    for d in range(16):
        flat[d * shard_rows : (d + 1) * shard_rows, :] = slots[d].astype(jnp.float32)[:shard_rows]

    per_up = value_width // LANES
    up_m = jnp.concatenate(
        [flat[pl.ds(down_rows + j, rank, stride=per_up), :] for j in range(per_up)], axis=1
    ).astype(jnp.bfloat16)
    own_rank = dot(up_ref[...], up_m, (1, 1)).astype(jnp.bfloat16)
    per_row = width // LANES

    def part(n, projected):
        cols = pl.ds(pl.multiple_of(n * CHUNK, CHUNK), CHUNK)
        rows = [pl.ds(n * (CHUNK // LANES) + j, rank, stride=per_row) for j in range(CHUNK // LANES)]
        d_part = jnp.concatenate([flat[r, :] for r in rows], axis=1).astype(jnp.bfloat16)
        down[:, cols] = d_part
        a_part = act_ref[:, cols]
        g_part = scale * dot(own_rank, a_part, (0, 0))
        for j, r in enumerate(rows):
            grad[r, :] = g_part[:, j * LANES : (j + 1) * LANES]
        return projected + dot(a_part, d_part, (1, 1))

    projected = lax.fori_loop(
        0, width // CHUNK, part, jnp.zeros((tokens, rank), jnp.float32)
    ).astype(jnp.bfloat16)
    g_up = scale * dot(projected, up_ref[...], (0, 0))
    for j in range(per_up):
        grad[pl.ds(down_rows + j, rank, stride=per_up), :] = g_up[:, j * LANES : (j + 1) * LANES]

    quarter = 4 * shard_rows

    def grad_rows(at):
        return pl.ds(pl.multiple_of(at * quarter, quarter), quarter)

    g_core_far = send(grad.at[grad_rows(o_diag)], from_core.at[0], core_dev)
    g_core_own = send(grad.at[grad_rows(o_core)], from_core.at[1], core_dev)
    pass_weight(1)
    u_core.wait_recv()
    u_far.wait_recv()
    u_rows = 4 * tokens
    rank_all = dot(up_all[...].reshape(u_rows, value_width), up_m, (1, 1)).astype(jnp.bfloat16)

    block_copies = []

    def block_math(k):
        first = pl.multiple_of((o * 4 + z_from[k]) * feats, feats)
        w = w_ref[...] if k == 0 else w_buf[k - 1]
        value = dot(up_all[...].reshape(u_rows, value_width), w, (1, 1)) + scale * dot(
            rank_all, down[:, pl.ds(first, feats)], (1, 0)
        )
        blocks[k] = value.astype(jnp.bfloat16).reshape(4, tokens, feats)
        out_ref[:, pl.ds(first, feats)] = blocks[k, o]

    def block_send(k):
        first = pl.multiple_of((o * 4 + z_from[k]) * feats, feats)
        for to, device in ((o_x, x_dev), (o_diag, diag_dev), (o_core, core_dev)):
            block_copies.append(
                send(blocks.at[k, to], out_ref.at[:, pl.ds(first, feats)], device)
            )

    block_math(0)
    g_core_far.wait_recv()
    half_sum[0] = grad[grad_rows(o_x), :] + from_core[0]
    g_x = send(half_sum.at[0], from_x, x_dev)
    block_send(0)
    g_core_own.wait_recv()
    half_sum[1] = grad[grad_rows(o), :] + from_core[1]
    pass_weight(2)
    w_y[1].wait_recv()
    block_math(1)
    block_send(1)
    g_x.wait_recv()
    half_sum[1] += from_x[...]

    def shard(at):
        return pl.ds(pl.multiple_of(at * shard_rows, shard_rows), shard_rows)

    g_z = [
        send(half_sum.at[1, shard(z_to[k])], from_z.at[k - 1], z_devs[k]) for k in range(1, 4)
    ]
    pass_weight(3)
    w_y[2].wait_recv()
    block_math(2)
    block_send(2)
    for copy in g_z:
        copy.wait_recv()
    total = half_sum[1, shard(z), :] + from_z[0] + from_z[1] + from_z[2]
    grad_total = total
    sq_own[...] = jnp.sum((total * total).reshape(shard_rows // 8, 8, LANES), axis=0)
    s_z = [send(sq_own, sq_z.at[k - 1], z_devs[k]) for k in range(1, 4)]
    w_y[3].wait_recv()
    block_math(3)
    block_send(3)
    for copy in s_z:
        copy.wait_recv()
    sq_line[...] = sq_own[...] + sq_z[0] + sq_z[1] + sq_z[2]
    s_s = [
        send(sq_line, sq_s.at[n], device)
        for n, device in enumerate((core_dev, x_dev, diag_dev))
    ]
    for copy in s_s:
        copy.wait_recv()
    sum_squares = jnp.sum(sq_line[...] + sq_s[0] + sq_s[1] + sq_s[2], keepdims=True)
    new_master_ref[...], new_moment_ref[...], new_second_ref[...] = adam(
        grad_total, sum_squares, master_ref[...], moment_ref[...], second_ref[...], params
    )
    for copy in block_copies:
        copy.wait_recv()
    for copy in used:
        copy.wait_send()


N_COPIES = 64


def fused(rank, activations, upstream, weight, master, moment, second_moment):
    tokens, width = activations.shape
    value_width = upstream.shape[1]
    feats = weight.shape[0]
    shard_rows = master.shape[0] // LANES
    flat_rows = 16 * shard_rows
    padded = -(-shard_rows // 16) * 16
    state = jax.ShapeDtypeStruct((shard_rows, LANES), jnp.float32)
    bf16, f32 = jnp.bfloat16, jnp.float32
    vmem = pl.BlockSpec(memory_space=pltpu.VMEM)
    result = pl.pallas_call(
        functools.partial(kernel, rank),
        out_shape=(jax.ShapeDtypeStruct((tokens, width), bf16), state, state, state),
        in_specs=[vmem] * 6,
        out_specs=(vmem,) * 4,
        scratch_shapes=[
            pltpu.VMEM((16, padded, LANES), bf16),
            pltpu.VMEM((flat_rows, LANES), f32),
            pltpu.VMEM((rank, width), bf16),
            pltpu.VMEM((4, tokens, value_width), bf16),
            pltpu.VMEM((3, feats, value_width), bf16),
            pltpu.VMEM((flat_rows, LANES), f32),
            pltpu.VMEM((2, 4 * shard_rows, LANES), f32),
            pltpu.VMEM((2, 4 * shard_rows, LANES), f32),
            pltpu.VMEM((4 * shard_rows, LANES), f32),
            pltpu.VMEM((3, shard_rows, LANES), f32),
            pltpu.VMEM((8, LANES), f32),
            pltpu.VMEM((3, 8, LANES), f32),
            pltpu.VMEM((8, LANES), f32),
            pltpu.VMEM((3, 8, LANES), f32),
            pltpu.VMEM((4, 4, tokens, feats), bf16),
            pltpu.SemaphoreType.DMA((N_COPIES,)),
            pltpu.SemaphoreType.DMA((N_COPIES,)),
        ],
        compiler_params=pltpu.CompilerParams(
            collective_id=0, has_side_effects=True, vmem_limit_bytes=52 * 1024 * 1024
        ),
        name="adapter_backward",
    )(
        activations,
        upstream,
        weight,
        master.reshape(shard_rows, LANES),
        moment.reshape(shard_rows, LANES),
        second_moment.reshape(shard_rows, LANES),
    )
    return (result[0],) + tuple(r.reshape(-1) for r in result[1:])


def solution(mesh):
    sizes = dict(mesh.shape)
    square = sizes["groups"] == 2 and sizes["outer"] == 4 and sizes["inner"] == 4

    def body(activations, upstream, weight, master, moment, second_moment):
        width, value_width = activations.shape[1], upstream.shape[1]
        rank = master.shape[0] * sizes["outer"] * sizes["inner"] // (width + value_width)
        fits = (
            activations.shape[0] % 16 == 0
            and width % CHUNK == 0
            and value_width % LANES == 0
            and weight.shape[0] % 256 == 0
            and master.shape[0] % (8 * LANES) == 0
            and rank % 16 == 0
        )
        if square and fits:
            return fused(rank, activations, upstream, weight, master, moment, second_moment)
        return per_device(activations, upstream, weight, master, moment, second_moment)

    return jax.shard_map(
        body,
        mesh=mesh,
        in_specs=(
            P(("groups", "outer", "inner"), None),
            P(("groups", "outer", "inner"), None),
            P(("outer", "inner"), None),
            P(("groups", "outer", "inner")),
            P(("groups", "outer", "inner")),
            P(("groups", "outer", "inner")),
        ),
        out_specs=(
            P(("groups", "outer", "inner"), None),
            P(("groups", "outer", "inner")),
            P(("groups", "outer", "inner")),
            P(("groups", "outer", "inner")),
        ),
        check_vma=False,
    )
```

```python
import functools
import math

import jax
import jax.numpy as jnp
from jax import lax
from jax.experimental import pallas as pl
from jax.experimental.pallas import tpu as pltpu
from jax.sharding import PartitionSpec as P

MESH = pl.DeviceIdType.MESH
LANES = 128
CHUNK = 1024


def per_device(activations, upstream, frozen_weight_matrix, master, moment, second_moment):
    width = activations.shape[1]
    value_width = upstream.shape[1]
    whole = lax.all_gather(master.astype(jnp.bfloat16), ("outer", "inner"), axis=0, tiled=True)
    rank_activations = whole.shape[0] // (width + value_width)
    adapter_scale_factor = 0.5 / math.sqrt(rank_activations * value_width)
    down_weight_transposed = whole[: rank_activations * width].reshape(rank_activations, width)
    up_m = whole[rank_activations * width :].reshape(rank_activations, value_width)
    rank_gradient = jnp.dot(upstream, up_m.T, preferred_element_type=jnp.float32).astype(
        jnp.bfloat16
    )
    projected_rows = jnp.dot(
        activations, down_weight_transposed.T, preferred_element_type=jnp.float32
    ).astype(jnp.bfloat16)
    down_weight_gradient = adapter_scale_factor * jnp.dot(
        rank_gradient.T, activations, preferred_element_type=jnp.float32
    )
    up_weight_gradient = adapter_scale_factor * jnp.dot(
        projected_rows.T, upstream, preferred_element_type=jnp.float32
    )
    flat_grad = jnp.concatenate([down_weight_gradient.reshape(-1), up_weight_gradient.reshape(-1)])
    grad_shard = lax.psum_scatter(flat_grad, ("outer", "inner"), scatter_dimension=0, tiled=True)
    sum_squares = lax.psum(jnp.sum(grad_shard * grad_shard), ("outer", "inner"))
    feat_rows = frozen_weight_matrix.shape[0]
    feat_start = lax.axis_index(("outer", "inner")) * feat_rows
    own_cols = lax.dynamic_slice_in_dim(down_weight_transposed, feat_start, feat_rows, 1)
    tok_piece = lax.all_gather(upstream, ("outer", "inner"), axis=0, tiled=True)
    rank_piece = jnp.dot(tok_piece, up_m.T, preferred_element_type=jnp.float32).astype(jnp.bfloat16)
    frozen_output = lax.dot_general(
        tok_piece,
        frozen_weight_matrix,
        (((1,), (1,)), ((), ())),
        preferred_element_type=jnp.float32,
    )
    feat_block = (
        frozen_output
        + adapter_scale_factor * jnp.dot(rank_piece, own_cols, preferred_element_type=jnp.float32)
    ).astype(jnp.bfloat16)
    n_outer = lax.axis_size("outer")
    n_inner = lax.axis_size("inner")
    tok_count = upstream.shape[0]
    reordered = (
        feat_block.reshape(n_outer, n_inner, tok_count, feat_rows)
        .transpose(1, 0, 2, 3)
        .reshape(n_inner * n_outer * tok_count, feat_rows)
    )
    input_gradient_rows = lax.all_to_all(
        lax.all_to_all(reordered, "inner", split_axis=0, concat_axis=1, tiled=True),
        "outer",
        split_axis=0,
        concat_axis=1,
        tiled=True,
    )
    norm = jnp.sqrt(sum_squares + 1e-06)
    clipped = grad_shard * jnp.minimum(1.0, math.sqrt(whole.shape[0]) / norm)
    return (input_gradient_rows,) + adam(clipped, master, moment, second_moment)


def adam(clipped, master, moment, second_moment):
    new_moment = 0.9 * moment + 0.1 * clipped
    new_second = 0.999 * second_moment + 0.001 * clipped * clipped
    corr_one = 1.0 - 0.9**10
    corr_two = 1.0 - 0.999**10
    new_master = master - 0.1 * (new_moment / corr_one) / (jnp.sqrt(new_second / corr_two) + 1e-08)
    return new_master, new_moment, new_second


def dot(a, b, contract):
    return lax.dot_general(
        a, b, (((contract[0],), (contract[1],)), ((), ())), preferred_element_type=jnp.float32
    )


def kernel(
    rank,
    act_hbm,
    up_hbm,
    w_hbm,
    master_hbm,
    out_ref,
    clipped_ref,
    act_ref,
    master_ref,
    slots,
    flat,
    down,
    up_all,
    w_buf,
    grad,
    from_core,
    half_sum,
    from_x,
    from_z,
    sq_own,
    sq_z,
    sq_line,
    sq_s,
    blocks,
    load_sem,
    send_sem,
    recv_sem,
    w_send_sem,
    w_recv_sem,
):
    y = lax.axis_index("groups")
    o = lax.axis_index("outer")
    z = lax.axis_index("inner")
    x, c = o // 2, lax.rem(o, 2)
    o_core = 2 * x + (1 - c)
    o_x = 2 * (1 - x) + c
    o_diag = 2 * (1 - x) + (1 - c)
    core_dev, x_dev, diag_dev = {"outer": o_core}, {"outer": o_x}, {"outer": o_diag}
    y_dev = {"groups": 1 - y}
    z_to = [None] + [lax.rem(z + k, 4) for k in range(1, 4)]
    z_from = [z] + [lax.rem(z + 4 - k, 4) for k in range(1, 4)]
    z_devs = [None] + [{"inner": z_to[k]} for k in range(1, 4)]
    high = z // 2
    u = z + high * (3 - 2 * z)
    order = [z] + [f + high * (3 - 2 * f) for f in (1 - u, 2, 3)]

    tokens, width = act_ref.shape
    value_width = up_all.shape[2]
    feats = w_buf.shape[1]
    half = feats // 2
    shard_rows = master_ref.shape[0]
    down_rows = rank * width // LANES
    params = 16 * shard_rows * LANES
    scale = 0.5 / math.sqrt(rank * value_width)

    barrier = pltpu.get_barrier_semaphore()
    partners = [core_dev, x_dev, diag_dev, y_dev] + z_devs[1:]
    for device in partners:
        pl.semaphore_signal(barrier, inc=1, device_id=device, device_id_type=MESH)

    loads = [
        pltpu.make_async_copy(src, dst, load_sem.at[n])
        for n, (src, dst) in enumerate(
            (
                (master_hbm, master_ref),
                (up_hbm, up_all.at[o]),
                (w_hbm, w_buf.at[z]),
                (act_hbm, act_ref),
            )
        )
    ]
    for load in loads:
        load.start()
    load_master, load_up, load_w, load_act = loads

    used = []

    def send(src, dst, device):
        at = len(used)
        copy = pltpu.make_async_remote_copy(
            src_ref=src,
            dst_ref=dst,
            send_sem=send_sem.at[at],
            recv_sem=recv_sem.at[at],
            device_id=device,
            device_id_type=MESH,
        )
        used.append(copy)
        copy.start()
        return copy

    own = o * 4 + z
    pad = slots.shape[1] - shard_rows
    load_master.wait()
    slots[own] = jnp.concatenate(
        [master_ref[...], jnp.zeros((pad, LANES), jnp.float32)], axis=0
    ).astype(jnp.bfloat16)
    pl.semaphore_wait(barrier, len(partners))

    my_half = pl.ds(pl.multiple_of(y * half, half), half)
    other_half = pl.ds(pl.multiple_of((1 - y) * half, half), half)

    def weight_copy(b, way, device):
        at = w_buf.at[b, my_half]
        return pltpu.make_async_remote_copy(
            src_ref=at,
            dst_ref=at,
            send_sem=w_send_sem.at[way, b],
            recv_sem=w_recv_sem.at[way // 2, b],
            device_id=device,
            device_id_type=MESH,
        )

    def weight_up(b):
        return weight_copy(b, 0, {"inner": z + 1})

    def weight_down(b):
        return weight_copy(b, 1, {"inner": z - 1})

    def weight_y(b):
        return weight_copy(b, 2, y_dev)

    goes_up = lambda b: (b <= z) & (z < 3)
    goes_down = lambda b: (b >= z) & (z > 0)

    def pass_on(b):
        pl.when(goes_up(b))(lambda: weight_up(b).start())
        pl.when(goes_down(b))(lambda: weight_down(b).start())

    def arrive(n):
        b = order[n]
        pltpu.make_async_remote_copy(
            src_ref=w_buf.at[b, my_half],
            dst_ref=w_buf.at[b, my_half],
            send_sem=w_send_sem.at[0, b],
            recv_sem=w_recv_sem.at[0, b],
            device_id=y_dev,
            device_id_type=MESH,
        ).wait_recv()
        pass_on(b)
        weight_y(b).start()

    slot_z = [None] + [send(slots.at[own], slots.at[own], z_devs[k]) for k in range(1, 4)]
    slot_x = [send(slots.at[own], slots.at[own], x_dev)]
    slot_core = [send(slots.at[own], slots.at[own], core_dev)]
    load_w.wait()
    pass_on(z)
    load_up.wait()
    u_x = send(up_all.at[o], up_all.at[o], x_dev)
    u_core = send(up_all.at[o], up_all.at[o], core_dev)
    for k in range(1, 4):
        slot_z[k].wait_recv()
        at = slots.at[o * 4 + z_from[k]]
        slot_x.append(send(at, at, x_dev))
        slot_core.append(send(at, at, core_dev))
    for k in range(4):
        slot_x[k].wait_recv()
        at = slots.at[o_x * 4 + z_from[k]]
        slot_core.append(send(at, at, core_dev))
    u_x.wait_recv()
    u_far = send(up_all.at[o_x], up_all.at[o_x], core_dev)
    middle = u == 1
    arrive(1)
    pl.when(middle)(lambda: arrive(2))

    for copy in slot_core:
        copy.wait_recv()
    for d in range(16):
        flat[d * shard_rows : (d + 1) * shard_rows, :] = slots[d].astype(jnp.float32)[:shard_rows]

    per_up = value_width // LANES
    up_m = jnp.concatenate(
        [flat[pl.ds(down_rows + j, rank, stride=per_up), :] for j in range(per_up)], axis=1
    ).astype(jnp.bfloat16)
    own_rank = dot(up_all[o], up_m, (1, 1)).astype(jnp.bfloat16)
    per_row = width // LANES
    load_act.wait()

    def part(n, projected):
        cols = pl.ds(pl.multiple_of(n * CHUNK, CHUNK), CHUNK)
        rows = [pl.ds(n * (CHUNK // LANES) + j, rank, stride=per_row) for j in range(CHUNK // LANES)]
        d_part = jnp.concatenate([flat[r, :] for r in rows], axis=1).astype(jnp.bfloat16)
        down[:, cols] = d_part
        a_part = act_ref[:, cols]
        g_part = scale * dot(own_rank, a_part, (0, 0))
        for j, r in enumerate(rows):
            grad[r, :] = g_part[:, j * LANES : (j + 1) * LANES]
        return projected + dot(a_part, d_part, (1, 1))

    projected = lax.fori_loop(
        0, width // CHUNK, part, jnp.zeros((tokens, rank), jnp.float32)
    ).astype(jnp.bfloat16)
    g_up = scale * dot(projected, up_all[o], (0, 0))
    for j in range(per_up):
        grad[pl.ds(down_rows + j, rank, stride=per_up), :] = g_up[:, j * LANES : (j + 1) * LANES]

    quarter = 4 * shard_rows

    def grad_rows(at):
        return pl.ds(pl.multiple_of(at * quarter, quarter), quarter)

    g_core_far = send(grad.at[grad_rows(o_diag)], from_core.at[0], core_dev)
    g_core_own = send(grad.at[grad_rows(o_core)], from_core.at[1], core_dev)
    u_core.wait_recv()
    u_far.wait_recv()
    u_rows = 4 * tokens
    rank_all = dot(up_all[...].reshape(u_rows, value_width), up_m, (1, 1)).astype(jnp.bfloat16)

    block_copies = []

    def block_cols(n):
        return pl.ds(pl.multiple_of((o * 4 + order[n]) * feats, feats), feats)

    def block_math(n):
        cols = block_cols(n)
        value = dot(up_all[...].reshape(u_rows, value_width), w_buf[order[n]], (1, 1))
        value += scale * dot(rank_all, down[:, cols], (1, 0))
        blocks[n] = value.astype(jnp.bfloat16).reshape(4, tokens, feats)
        out_ref[:, cols] = blocks[n, o]

    def block_send(n):
        for to, device in ((o_x, x_dev), (o_diag, diag_dev), (o_core, core_dev)):
            block_copies.append(send(blocks.at[n, to], out_ref.at[:, block_cols(n)], device))

    def weight_ready(n):
        b = order[n]
        pltpu.make_async_remote_copy(
            src_ref=w_buf.at[b, other_half],
            dst_ref=w_buf.at[b, other_half],
            send_sem=w_send_sem.at[2, b],
            recv_sem=w_recv_sem.at[1, b],
            device_id=y_dev,
            device_id_type=MESH,
        ).wait_recv()

    block_math(0)
    g_core_far.wait_recv()
    half_sum[0] = grad[grad_rows(o_x), :] + from_core[0]
    g_x = send(half_sum.at[0], from_x, x_dev)
    block_send(0)
    g_core_own.wait_recv()
    half_sum[1] = grad[grad_rows(o), :] + from_core[1]
    pl.when(middle)(lambda: arrive(3))
    pl.when(jnp.logical_not(middle))(lambda: arrive(2))
    weight_ready(1)
    block_math(1)
    block_send(1)
    g_x.wait_recv()
    half_sum[1] += from_x[...]

    def shard(at):
        return pl.ds(pl.multiple_of(at * shard_rows, shard_rows), shard_rows)

    g_z = [
        send(half_sum.at[1, shard(z_to[k])], from_z.at[k - 1], z_devs[k]) for k in range(1, 4)
    ]
    pl.when(jnp.logical_not(middle))(lambda: arrive(3))
    weight_ready(2)
    block_math(2)
    block_send(2)
    for copy in g_z:
        copy.wait_recv()
    total = half_sum[1, shard(z), :] + from_z[0] + from_z[1] + from_z[2]
    clipped_ref[...] = total
    sq_own[...] = jnp.sum((total * total).reshape(shard_rows // 8, 8, LANES), axis=0)
    s_z = [send(sq_own, sq_z.at[k - 1], z_devs[k]) for k in range(1, 4)]
    weight_ready(3)
    block_math(3)
    block_send(3)
    for copy in s_z:
        copy.wait_recv()
    sq_line[...] = sq_own[...] + sq_z[0] + sq_z[1] + sq_z[2]
    s_s = [
        send(sq_line, sq_s.at[n], device)
        for n, device in enumerate((core_dev, x_dev, diag_dev))
    ]
    for copy in s_s:
        copy.wait_recv()
    sum_squares = jnp.sum(sq_line[...] + sq_s[0] + sq_s[1] + sq_s[2], keepdims=True)
    norm = jnp.sqrt(sum_squares + 1e-06)
    clipped_ref[...] = clipped_ref[...] * jnp.minimum(1.0, math.sqrt(params) / norm)
    for copy in block_copies:
        copy.wait_recv()
    for copy in used:
        copy.wait_send()
    for n in range(4):
        b = order[n]
        pl.when(goes_up(b))(lambda b=b: weight_up(b).wait_send())
        pl.when(goes_down(b))(lambda b=b: weight_down(b).wait_send())
        if n > 0:
            weight_y(b).wait_send()


N_COPIES = 64


def fused(rank, activations, upstream, weight, master, moment, second_moment):
    tokens, width = activations.shape
    value_width = upstream.shape[1]
    feats = weight.shape[0]
    shard_rows = master.shape[0] // LANES
    flat_rows = 16 * shard_rows
    padded = -(-shard_rows // 16) * 16
    state = jax.ShapeDtypeStruct((shard_rows, LANES), jnp.float32)
    bf16, f32 = jnp.bfloat16, jnp.float32
    vmem = pl.BlockSpec(memory_space=pltpu.VMEM)
    hbm = pl.BlockSpec(memory_space=pltpu.HBM)
    rows, clipped = pl.pallas_call(
        functools.partial(kernel, rank),
        out_shape=(jax.ShapeDtypeStruct((tokens, width), bf16), state),
        in_specs=[hbm] * 4,
        out_specs=(vmem,) * 2,
        scratch_shapes=[
            pltpu.VMEM((tokens, width), bf16),
            pltpu.VMEM((shard_rows, LANES), f32),
            pltpu.VMEM((16, padded, LANES), bf16),
            pltpu.VMEM((flat_rows, LANES), f32),
            pltpu.VMEM((rank, width), bf16),
            pltpu.VMEM((4, tokens, value_width), bf16),
            pltpu.VMEM((4, feats, value_width), bf16),
            pltpu.VMEM((flat_rows, LANES), f32),
            pltpu.VMEM((2, 4 * shard_rows, LANES), f32),
            pltpu.VMEM((2, 4 * shard_rows, LANES), f32),
            pltpu.VMEM((4 * shard_rows, LANES), f32),
            pltpu.VMEM((3, shard_rows, LANES), f32),
            pltpu.VMEM((8, LANES), f32),
            pltpu.VMEM((3, 8, LANES), f32),
            pltpu.VMEM((8, LANES), f32),
            pltpu.VMEM((3, 8, LANES), f32),
            pltpu.VMEM((4, 4, tokens, feats), bf16),
            pltpu.SemaphoreType.DMA((4,)),
            pltpu.SemaphoreType.DMA((N_COPIES,)),
            pltpu.SemaphoreType.DMA((N_COPIES,)),
            pltpu.SemaphoreType.DMA((3, 4)),
            pltpu.SemaphoreType.DMA((2, 4)),
        ],
        compiler_params=pltpu.CompilerParams(
            collective_id=0, has_side_effects=True, vmem_limit_bytes=56 * 1024 * 1024
        ),
        name="adapter_backward",
    )(activations, upstream, weight, master.reshape(shard_rows, LANES))
    return (rows,) + adam(clipped.reshape(-1), master, moment, second_moment)


def solution(mesh):
    sizes = dict(mesh.shape)
    square = sizes["groups"] == 2 and sizes["outer"] == 4 and sizes["inner"] == 4

    def body(activations, upstream, weight, master, moment, second_moment):
        width, value_width = activations.shape[1], upstream.shape[1]
        rank = master.shape[0] * sizes["outer"] * sizes["inner"] // (width + value_width)
        fits = (
            activations.shape[0] % 16 == 0
            and width % CHUNK == 0
            and value_width % LANES == 0
            and weight.shape[0] % 256 == 0
            and master.shape[0] % (8 * LANES) == 0
            and rank % 16 == 0
        )
        if square and fits:
            return fused(rank, activations, upstream, weight, master, moment, second_moment)
        return per_device(activations, upstream, weight, master, moment, second_moment)

    return jax.shard_map(
        body,
        mesh=mesh,
        in_specs=(
            P(("groups", "outer", "inner"), None),
            P(("groups", "outer", "inner"), None),
            P(("outer", "inner"), None),
            P(("groups", "outer", "inner")),
            P(("groups", "outer", "inner")),
            P(("groups", "outer", "inner")),
        ),
        out_specs=(
            P(("groups", "outer", "inner"), None),
            P(("groups", "outer", "inner")),
            P(("groups", "outer", "inner")),
            P(("groups", "outer", "inner")),
        ),
        check_vma=False,
    )
```

```python
import functools
import math

import jax
import jax.numpy as jnp
from jax import lax
from jax.experimental import pallas as pl
from jax.experimental.pallas import tpu as pltpu
from jax.sharding import PartitionSpec as P

MESH = pl.DeviceIdType.MESH
LANES = 128
CHUNK = 1024


def per_device(activations, upstream, frozen_weight_matrix, master, moment, second_moment):
    width = activations.shape[1]
    value_width = upstream.shape[1]
    whole = lax.all_gather(master.astype(jnp.bfloat16), ("outer", "inner"), axis=0, tiled=True)
    rank_activations = whole.shape[0] // (width + value_width)
    adapter_scale_factor = 0.5 / math.sqrt(rank_activations * value_width)
    down_weight_transposed = whole[: rank_activations * width].reshape(rank_activations, width)
    up_m = whole[rank_activations * width :].reshape(rank_activations, value_width)
    rank_gradient = jnp.dot(upstream, up_m.T, preferred_element_type=jnp.float32).astype(
        jnp.bfloat16
    )
    projected_rows = jnp.dot(
        activations, down_weight_transposed.T, preferred_element_type=jnp.float32
    ).astype(jnp.bfloat16)
    down_weight_gradient = adapter_scale_factor * jnp.dot(
        rank_gradient.T, activations, preferred_element_type=jnp.float32
    )
    up_weight_gradient = adapter_scale_factor * jnp.dot(
        projected_rows.T, upstream, preferred_element_type=jnp.float32
    )
    flat_grad = jnp.concatenate([down_weight_gradient.reshape(-1), up_weight_gradient.reshape(-1)])
    grad_shard = lax.psum_scatter(flat_grad, ("outer", "inner"), scatter_dimension=0, tiled=True)
    sum_squares = lax.psum(jnp.sum(grad_shard * grad_shard), ("outer", "inner"))
    feat_rows = frozen_weight_matrix.shape[0]
    feat_start = lax.axis_index(("outer", "inner")) * feat_rows
    own_cols = lax.dynamic_slice_in_dim(down_weight_transposed, feat_start, feat_rows, 1)
    tok_piece = lax.all_gather(upstream, ("outer", "inner"), axis=0, tiled=True)
    rank_piece = jnp.dot(tok_piece, up_m.T, preferred_element_type=jnp.float32).astype(jnp.bfloat16)
    frozen_output = lax.dot_general(
        tok_piece,
        frozen_weight_matrix,
        (((1,), (1,)), ((), ())),
        preferred_element_type=jnp.float32,
    )
    feat_block = (
        frozen_output
        + adapter_scale_factor * jnp.dot(rank_piece, own_cols, preferred_element_type=jnp.float32)
    ).astype(jnp.bfloat16)
    n_outer = lax.axis_size("outer")
    n_inner = lax.axis_size("inner")
    tok_count = upstream.shape[0]
    reordered = (
        feat_block.reshape(n_outer, n_inner, tok_count, feat_rows)
        .transpose(1, 0, 2, 3)
        .reshape(n_inner * n_outer * tok_count, feat_rows)
    )
    input_gradient_rows = lax.all_to_all(
        lax.all_to_all(reordered, "inner", split_axis=0, concat_axis=1, tiled=True),
        "outer",
        split_axis=0,
        concat_axis=1,
        tiled=True,
    )
    norm = jnp.sqrt(sum_squares + 1e-06)
    clipped = grad_shard * jnp.minimum(1.0, math.sqrt(whole.shape[0]) / norm)
    return (input_gradient_rows,) + adam(clipped, master, moment, second_moment)


def adam(clipped, master, moment, second_moment):
    new_moment = 0.9 * moment + 0.1 * clipped
    new_second = 0.999 * second_moment + 0.001 * clipped * clipped
    corr_one = 1.0 - 0.9**10
    corr_two = 1.0 - 0.999**10
    new_master = master - 0.1 * (new_moment / corr_one) / (jnp.sqrt(new_second / corr_two) + 1e-08)
    return new_master, new_moment, new_second


def dot(a, b, contract):
    return lax.dot_general(
        a, b, (((contract[0],), (contract[1],)), ((), ())), preferred_element_type=jnp.float32
    )


def kernel(
    rank,
    act_hbm,
    up_hbm,
    w_hbm,
    master_hbm,
    out_ref,
    clipped_ref,
    act_ref,
    master_ref,
    slots,
    flat,
    down,
    up_all,
    w_buf,
    grad,
    from_core,
    half_sum,
    from_x,
    from_z,
    sq_own,
    sq_z,
    sq_line,
    sq_s,
    blocks,
    load_sem,
    send_sem,
    recv_sem,
    w_send_sem,
    w_recv_sem,
):
    y = lax.axis_index("groups")
    o = lax.axis_index("outer")
    z = lax.axis_index("inner")
    x, c = o // 2, lax.rem(o, 2)
    o_core = 2 * x + (1 - c)
    o_x = 2 * (1 - x) + c
    o_diag = 2 * (1 - x) + (1 - c)
    core_dev, x_dev, diag_dev = {"outer": o_core}, {"outer": o_x}, {"outer": o_diag}
    y_dev = {"groups": 1 - y}
    z_to = [None] + [lax.rem(z + k, 4) for k in range(1, 4)]
    z_from = [z] + [lax.rem(z + 4 - k, 4) for k in range(1, 4)]
    z_devs = [None] + [{"inner": z_to[k]} for k in range(1, 4)]
    high = z // 2
    u = z + high * (3 - 2 * z)
    order = [z] + [f + high * (3 - 2 * f) for f in (1 - u, 2, 3)]

    tokens, width = act_ref.shape
    value_width = up_all.shape[2]
    feats = w_buf.shape[1]
    half = feats // 2
    shard_rows = master_ref.shape[0]
    down_rows = rank * width // LANES
    params = 16 * shard_rows * LANES
    scale = 0.5 / math.sqrt(rank * value_width)

    barrier = pltpu.get_barrier_semaphore()
    partners = [core_dev, x_dev, diag_dev, y_dev] + z_devs[1:]
    for device in partners:
        pl.semaphore_signal(barrier, inc=1, device_id=device, device_id_type=MESH)

    loads = [
        pltpu.make_async_copy(src, dst, load_sem.at[n])
        for n, (src, dst) in enumerate(
            (
                (master_hbm, master_ref),
                (up_hbm, up_all.at[o]),
                (w_hbm, w_buf.at[z]),
                (act_hbm, act_ref),
            )
        )
    ]
    for load in loads:
        load.start()
    load_master, load_up, load_w, load_act = loads

    used = []

    def send(src, dst, device):
        at = len(used)
        copy = pltpu.make_async_remote_copy(
            src_ref=src,
            dst_ref=dst,
            send_sem=send_sem.at[at],
            recv_sem=recv_sem.at[at],
            device_id=device,
            device_id_type=MESH,
        )
        used.append(copy)
        copy.start()
        return copy

    own = o * 4 + z
    pad = slots.shape[1] - shard_rows
    load_master.wait()
    slots[own] = jnp.concatenate(
        [master_ref[...], jnp.zeros((pad, LANES), jnp.float32)], axis=0
    ).astype(jnp.bfloat16)
    pl.semaphore_wait(barrier, len(partners))

    my_half = pl.ds(pl.multiple_of(y * half, half), half)
    other_half = pl.ds(pl.multiple_of((1 - y) * half, half), half)

    def weight_copy(b, way, device):
        at = w_buf.at[b, my_half]
        return pltpu.make_async_remote_copy(
            src_ref=at,
            dst_ref=at,
            send_sem=w_send_sem.at[way, b],
            recv_sem=w_recv_sem.at[way // 2, b],
            device_id=device,
            device_id_type=MESH,
        )

    def weight_up(b):
        return weight_copy(b, 0, {"inner": z + 1})

    def weight_down(b):
        return weight_copy(b, 1, {"inner": z - 1})

    def weight_y(b):
        return weight_copy(b, 2, y_dev)

    goes_up = lambda b: (b <= z) & (z < 3)
    goes_down = lambda b: (b >= z) & (z > 0)

    def pass_on(b):
        pl.when(goes_up(b))(lambda: weight_up(b).start())
        pl.when(goes_down(b))(lambda: weight_down(b).start())

    def arrive(n):
        b = order[n]
        pltpu.make_async_remote_copy(
            src_ref=w_buf.at[b, my_half],
            dst_ref=w_buf.at[b, my_half],
            send_sem=w_send_sem.at[0, b],
            recv_sem=w_recv_sem.at[0, b],
            device_id=y_dev,
            device_id_type=MESH,
        ).wait_recv()
        pass_on(b)
        weight_y(b).start()

    slot_z = [None] + [send(slots.at[own], slots.at[own], z_devs[k]) for k in range(1, 4)]
    slot_x = [send(slots.at[own], slots.at[own], x_dev)]
    slot_core = [send(slots.at[own], slots.at[own], core_dev)]
    load_up.wait()
    u_x = send(up_all.at[o], up_all.at[o], x_dev)
    u_core = send(up_all.at[o], up_all.at[o], core_dev)
    for k in range(1, 4):
        slot_z[k].wait_recv()
        at = slots.at[o * 4 + z_from[k]]
        slot_x.append(send(at, at, x_dev))
        slot_core.append(send(at, at, core_dev))
    load_w.wait()
    pass_on(z)
    for k in range(4):
        slot_x[k].wait_recv()
        at = slots.at[o_x * 4 + z_from[k]]
        slot_core.append(send(at, at, core_dev))
    u_x.wait_recv()
    u_far = send(up_all.at[o_x], up_all.at[o_x], core_dev)
    for copy in slot_core:
        copy.wait_recv()
    for d in range(16):
        flat[d * shard_rows : (d + 1) * shard_rows, :] = slots[d].astype(jnp.float32)[:shard_rows]

    per_up = value_width // LANES
    up_m = jnp.concatenate(
        [flat[pl.ds(down_rows + j, rank, stride=per_up), :] for j in range(per_up)], axis=1
    ).astype(jnp.bfloat16)
    per_row = width // LANES
    for j in range(per_row):
        row = flat[pl.ds(j, rank, stride=per_row), :]
        down[:, j * LANES : (j + 1) * LANES] = row.astype(jnp.bfloat16)

    u_core.wait_recv()
    u_far.wait_recv()
    u_rows = 4 * tokens
    rank_all = dot(up_all[...].reshape(u_rows, value_width), up_m, (1, 1)).astype(jnp.bfloat16)

    block_copies = []

    def block_cols(n):
        return pl.ds(pl.multiple_of((o * 4 + order[n]) * feats, feats), feats)

    def block_math(n):
        cols = block_cols(n)
        value = dot(up_all[...].reshape(u_rows, value_width), w_buf[order[n]], (1, 1))
        value += scale * dot(rank_all, down[:, cols], (1, 0))
        blocks[n] = value.astype(jnp.bfloat16).reshape(4, tokens, feats)
        out_ref[:, cols] = blocks[n, o]

    def block_send(n):
        for to, device in ((o_x, x_dev), (o_diag, diag_dev), (o_core, core_dev)):
            block_copies.append(send(blocks.at[n, to], out_ref.at[:, block_cols(n)], device))

    def weight_ready(n):
        b = order[n]
        pltpu.make_async_remote_copy(
            src_ref=w_buf.at[b, other_half],
            dst_ref=w_buf.at[b, other_half],
            send_sem=w_send_sem.at[2, b],
            recv_sem=w_recv_sem.at[1, b],
            device_id=y_dev,
            device_id_type=MESH,
        ).wait_recv()

    block_math(0)
    block_send(0)

    own_rank_t = jnp.transpose(dot(up_all[o], up_m, (1, 1))).astype(jnp.bfloat16)
    load_act.wait()

    def part(n, projected):
        cols = pl.ds(pl.multiple_of(n * CHUNK, CHUNK), CHUNK)
        a_part = act_ref[:, cols]
        g_part = scale * dot(own_rank_t, a_part, (1, 0))
        for j in range(CHUNK // LANES):
            at = pl.ds(n * (CHUNK // LANES) + j, rank, stride=per_row)
            grad[at, :] = g_part[:, j * LANES : (j + 1) * LANES]
        return projected + dot(a_part, down[:, cols], (1, 1))

    projected = lax.fori_loop(
        0, width // CHUNK, part, jnp.zeros((tokens, rank), jnp.float32)
    ).astype(jnp.bfloat16)
    g_up = scale * dot(projected, up_all[o], (0, 0))
    for j in range(per_up):
        grad[pl.ds(down_rows + j, rank, stride=per_up), :] = g_up[:, j * LANES : (j + 1) * LANES]

    quarter = 4 * shard_rows

    def grad_rows(at):
        return pl.ds(pl.multiple_of(at * quarter, quarter), quarter)

    g_core_far = send(grad.at[grad_rows(o_diag)], from_core.at[0], core_dev)
    g_core_own = send(grad.at[grad_rows(o_core)], from_core.at[1], core_dev)
    middle = u == 1
    g_core_far.wait_recv()
    half_sum[0] = grad[grad_rows(o_x), :] + from_core[0]
    g_x = send(half_sum.at[0], from_x, x_dev)
    arrive(1)
    pl.when(middle)(lambda: arrive(2))
    g_core_own.wait_recv()
    half_sum[1] = grad[grad_rows(o), :] + from_core[1]
    pl.when(middle)(lambda: arrive(3))
    pl.when(jnp.logical_not(middle))(lambda: arrive(2))
    weight_ready(1)
    block_math(1)
    g_x.wait_recv()
    half_sum[1] += from_x[...]

    def shard(at):
        return pl.ds(pl.multiple_of(at * shard_rows, shard_rows), shard_rows)

    g_z = [
        send(half_sum.at[1, shard(z_to[k])], from_z.at[k - 1], z_devs[k]) for k in range(1, 4)
    ]
    block_send(1)
    pl.when(jnp.logical_not(middle))(lambda: arrive(3))
    weight_ready(2)
    block_math(2)
    block_send(2)
    for copy in g_z:
        copy.wait_recv()
    total = half_sum[1, shard(z), :] + from_z[0] + from_z[1] + from_z[2]
    clipped_ref[...] = total
    sq_own[...] = jnp.sum((total * total).reshape(shard_rows // 8, 8, LANES), axis=0)
    s_z = [send(sq_own, sq_z.at[k - 1], z_devs[k]) for k in range(1, 4)]
    weight_ready(3)
    block_math(3)
    block_send(3)
    for copy in s_z:
        copy.wait_recv()
    sq_line[...] = sq_own[...] + sq_z[0] + sq_z[1] + sq_z[2]
    s_s = [
        send(sq_line, sq_s.at[n], device)
        for n, device in enumerate((core_dev, x_dev, diag_dev))
    ]
    for copy in s_s:
        copy.wait_recv()
    sum_squares = jnp.sum(sq_line[...] + sq_s[0] + sq_s[1] + sq_s[2], keepdims=True)
    norm = jnp.sqrt(sum_squares + 1e-06)
    clipped_ref[...] = clipped_ref[...] * jnp.minimum(1.0, math.sqrt(params) / norm)
    for copy in block_copies:
        copy.wait_recv()
    for copy in used:
        copy.wait_send()
    for n in range(4):
        b = order[n]
        pl.when(goes_up(b))(lambda b=b: weight_up(b).wait_send())
        pl.when(goes_down(b))(lambda b=b: weight_down(b).wait_send())
        if n > 0:
            weight_y(b).wait_send()


N_COPIES = 64


def fused(rank, activations, upstream, weight, master, moment, second_moment):
    tokens, width = activations.shape
    value_width = upstream.shape[1]
    feats = weight.shape[0]
    shard_rows = master.shape[0] // LANES
    flat_rows = 16 * shard_rows
    padded = -(-shard_rows // 16) * 16
    state = jax.ShapeDtypeStruct((shard_rows, LANES), jnp.float32)
    bf16, f32 = jnp.bfloat16, jnp.float32
    vmem = pl.BlockSpec(memory_space=pltpu.VMEM)
    hbm = pl.BlockSpec(memory_space=pltpu.HBM)
    rows, clipped = pl.pallas_call(
        functools.partial(kernel, rank),
        out_shape=(jax.ShapeDtypeStruct((tokens, width), bf16), state),
        in_specs=[hbm] * 4,
        out_specs=(vmem,) * 2,
        scratch_shapes=[
            pltpu.VMEM((tokens, width), bf16),
            pltpu.VMEM((shard_rows, LANES), f32),
            pltpu.VMEM((16, padded, LANES), bf16),
            pltpu.VMEM((flat_rows, LANES), f32),
            pltpu.VMEM((rank, width), bf16),
            pltpu.VMEM((4, tokens, value_width), bf16),
            pltpu.VMEM((4, feats, value_width), bf16),
            pltpu.VMEM((flat_rows, LANES), f32),
            pltpu.VMEM((2, 4 * shard_rows, LANES), f32),
            pltpu.VMEM((2, 4 * shard_rows, LANES), f32),
            pltpu.VMEM((4 * shard_rows, LANES), f32),
            pltpu.VMEM((3, shard_rows, LANES), f32),
            pltpu.VMEM((8, LANES), f32),
            pltpu.VMEM((3, 8, LANES), f32),
            pltpu.VMEM((8, LANES), f32),
            pltpu.VMEM((3, 8, LANES), f32),
            pltpu.VMEM((4, 4, tokens, feats), bf16),
            pltpu.SemaphoreType.DMA((4,)),
            pltpu.SemaphoreType.DMA((N_COPIES,)),
            pltpu.SemaphoreType.DMA((N_COPIES,)),
            pltpu.SemaphoreType.DMA((3, 4)),
            pltpu.SemaphoreType.DMA((2, 4)),
        ],
        compiler_params=pltpu.CompilerParams(
            collective_id=0, has_side_effects=True, vmem_limit_bytes=56 * 1024 * 1024
        ),
        name="adapter_backward",
    )(activations, upstream, weight, master.reshape(shard_rows, LANES))
    return (rows,) + adam(clipped.reshape(-1), master, moment, second_moment)


def solution(mesh):
    sizes = dict(mesh.shape)
    square = sizes["groups"] == 2 and sizes["outer"] == 4 and sizes["inner"] == 4

    def body(activations, upstream, weight, master, moment, second_moment):
        width, value_width = activations.shape[1], upstream.shape[1]
        rank = master.shape[0] * sizes["outer"] * sizes["inner"] // (width + value_width)
        fits = (
            activations.shape[0] % 16 == 0
            and width % CHUNK == 0
            and value_width % LANES == 0
            and weight.shape[0] % 256 == 0
            and master.shape[0] % (8 * LANES) == 0
            and rank % 16 == 0
        )
        if square and fits:
            return fused(rank, activations, upstream, weight, master, moment, second_moment)
        return per_device(activations, upstream, weight, master, moment, second_moment)

    return jax.shard_map(
        body,
        mesh=mesh,
        in_specs=(
            P(("groups", "outer", "inner"), None),
            P(("groups", "outer", "inner"), None),
            P(("outer", "inner"), None),
            P(("groups", "outer", "inner")),
            P(("groups", "outer", "inner")),
            P(("groups", "outer", "inner")),
        ),
        out_specs=(
            P(("groups", "outer", "inner"), None),
            P(("groups", "outer", "inner")),
            P(("groups", "outer", "inner")),
            P(("groups", "outer", "inner")),
        ),
        check_vma=False,
    )
```

```python
import functools
import math

import jax
import jax.numpy as jnp
from jax import lax
from jax.experimental import pallas as pl
from jax.experimental.pallas import tpu as pltpu
from jax.sharding import PartitionSpec as P

MESH = pl.DeviceIdType.MESH
LANES = 128
CHUNK = 1024
PIECES = 2
ROW_COPIES = 8
VMEM_GRANT = 56 * 1024 * 1024


def per_device(activations, upstream, frozen_weight_matrix, master, moment, second_moment):
    width = activations.shape[1]
    value_width = upstream.shape[1]
    whole = lax.all_gather(master.astype(jnp.bfloat16), ("outer", "inner"), axis=0, tiled=True)
    rank_activations = whole.shape[0] // (width + value_width)
    adapter_scale_factor = 0.5 / math.sqrt(rank_activations * value_width)
    down_weight_transposed = whole[: rank_activations * width].reshape(rank_activations, width)
    up_m = whole[rank_activations * width :].reshape(rank_activations, value_width)
    rank_gradient = jnp.dot(upstream, up_m.T, preferred_element_type=jnp.float32).astype(
        jnp.bfloat16
    )
    projected_rows = jnp.dot(
        activations, down_weight_transposed.T, preferred_element_type=jnp.float32
    ).astype(jnp.bfloat16)
    down_weight_gradient = adapter_scale_factor * jnp.dot(
        rank_gradient.T, activations, preferred_element_type=jnp.float32
    )
    up_weight_gradient = adapter_scale_factor * jnp.dot(
        projected_rows.T, upstream, preferred_element_type=jnp.float32
    )
    flat_grad = jnp.concatenate([down_weight_gradient.reshape(-1), up_weight_gradient.reshape(-1)])
    grad_shard = lax.psum_scatter(flat_grad, ("outer", "inner"), scatter_dimension=0, tiled=True)
    sum_squares = lax.psum(jnp.sum(grad_shard * grad_shard), ("outer", "inner"))
    feat_rows = frozen_weight_matrix.shape[0]
    feat_start = lax.axis_index(("outer", "inner")) * feat_rows
    own_cols = lax.dynamic_slice_in_dim(down_weight_transposed, feat_start, feat_rows, 1)
    tok_piece = lax.all_gather(upstream, ("outer", "inner"), axis=0, tiled=True)
    rank_piece = jnp.dot(tok_piece, up_m.T, preferred_element_type=jnp.float32).astype(jnp.bfloat16)
    frozen_output = lax.dot_general(
        tok_piece,
        frozen_weight_matrix,
        (((1,), (1,)), ((), ())),
        preferred_element_type=jnp.float32,
    )
    feat_block = (
        frozen_output
        + adapter_scale_factor * jnp.dot(rank_piece, own_cols, preferred_element_type=jnp.float32)
    ).astype(jnp.bfloat16)
    n_outer = lax.axis_size("outer")
    n_inner = lax.axis_size("inner")
    tok_count = upstream.shape[0]
    reordered = (
        feat_block.reshape(n_outer, n_inner, tok_count, feat_rows)
        .transpose(1, 0, 2, 3)
        .reshape(n_inner * n_outer * tok_count, feat_rows)
    )
    input_gradient_rows = lax.all_to_all(
        lax.all_to_all(reordered, "inner", split_axis=0, concat_axis=1, tiled=True),
        "outer",
        split_axis=0,
        concat_axis=1,
        tiled=True,
    )
    norm = jnp.sqrt(sum_squares + 1e-06)
    clipped = grad_shard * jnp.minimum(1.0, math.sqrt(whole.shape[0]) / norm)
    return (input_gradient_rows,) + adam(clipped, master, moment, second_moment)


def adam(clipped, master, moment, second_moment):
    new_moment = 0.9 * moment + 0.1 * clipped
    new_second = 0.999 * second_moment + 0.001 * clipped * clipped
    corr_one = 1.0 - 0.9**10
    corr_two = 1.0 - 0.999**10
    new_master = master - 0.1 * (new_moment / corr_one) / (jnp.sqrt(new_second / corr_two) + 1e-08)
    return new_master, new_moment, new_second


def dot(a, b, contract):
    return lax.dot_general(
        a, b, (((contract[0],), (contract[1],)), ((), ())), preferred_element_type=jnp.float32
    )


def kernel(
    rank,
    act_hbm,
    up_hbm,
    w_hbm,
    master_hbm,
    out_ref,
    clipped_ref,
    act_ref,
    master_ref,
    slots,
    flat,
    up_all,
    w_buf,
    grad,
    from_core,
    half_sum,
    from_x,
    from_z,
    sq_own,
    sq_z,
    sq_line,
    sq_s,
    blocks,
    load_sem,
    send_sem,
    recv_sem,
    w_send_sem,
    w_recv_sem,
):
    y = lax.axis_index("groups")
    o = lax.axis_index("outer")
    z = lax.axis_index("inner")
    x, c = o // 2, lax.rem(o, 2)
    o_core = 2 * x + (1 - c)
    o_x = 2 * (1 - x) + c
    o_diag = 2 * (1 - x) + (1 - c)
    core_dev, x_dev, diag_dev = {"outer": o_core}, {"outer": o_x}, {"outer": o_diag}
    y_dev = {"groups": 1 - y}
    z_to = [None] + [lax.rem(z + k, 4) for k in range(1, 4)]
    z_from = [z] + [lax.rem(z + 4 - k, 4) for k in range(1, 4)]
    z_devs = [None] + [{"inner": z_to[k]} for k in range(1, 4)]
    high = z // 2
    u = z + high * (3 - 2 * z)
    order = [z] + [f + high * (3 - 2 * f) for f in (1 - u, 2, 3)]

    tokens, width = act_ref.shape
    value_width = up_all.shape[2]
    feats = w_buf.shape[1]
    half = feats // 2
    shard_rows = master_ref.shape[0]
    down_rows = rank * width // LANES
    params = 16 * shard_rows * LANES
    scale = 0.5 / math.sqrt(rank * value_width)

    barrier = pltpu.get_barrier_semaphore()
    partners = [core_dev, x_dev, diag_dev, y_dev] + z_devs[1:]
    for device in partners:
        pl.semaphore_signal(barrier, inc=1, device_id=device, device_id_type=MESH)

    loads = [
        pltpu.make_async_copy(src, dst, load_sem.at[n])
        for n, (src, dst) in enumerate(
            (
                (master_hbm, master_ref),
                (up_hbm, up_all.at[o]),
                (w_hbm, w_buf.at[z]),
                (act_hbm, act_ref),
            )
        )
    ]
    for load in loads:
        load.start()
    load_master, load_up, load_w, load_act = loads

    used = []

    def send(src, dst, device):
        at = len(used)
        copy = pltpu.make_async_remote_copy(
            src_ref=src,
            dst_ref=dst,
            send_sem=send_sem.at[at],
            recv_sem=recv_sem.at[at],
            device_id=device,
            device_id_type=MESH,
        )
        used.append(copy)
        copy.start()
        return copy

    own = o * 4 + z
    pad = slots.shape[1] - shard_rows
    load_master.wait()
    slots[own] = jnp.concatenate(
        [master_ref[...], jnp.zeros((pad, LANES), jnp.float32)], axis=0
    ).astype(jnp.bfloat16)
    pl.semaphore_wait(barrier, len(partners))

    piece = half // PIECES

    def weight_rows(part_y, m):
        return pl.ds(pl.multiple_of(part_y * half + m * piece, piece), piece)

    def weight_copy(b, m, part_y, way, device):
        at = w_buf.at[b, weight_rows(part_y, m)]
        return pltpu.make_async_remote_copy(
            src_ref=at,
            dst_ref=at,
            send_sem=w_send_sem.at[way, m, b],
            recv_sem=w_recv_sem.at[way // 2, m, b],
            device_id=device,
            device_id_type=MESH,
        )

    def weight_up(b, m):
        return weight_copy(b, m, y, 0, {"inner": z + 1})

    def weight_down(b, m):
        return weight_copy(b, m, y, 1, {"inner": z - 1})

    def weight_y(b, m):
        return weight_copy(b, m, y, 2, y_dev)

    goes_up = lambda b: (b <= z) & (z < 3)
    goes_down = lambda b: (b >= z) & (z > 0)

    def pass_on(b, m):
        pl.when(goes_up(b))(lambda: weight_up(b, m).start())
        pl.when(goes_down(b))(lambda: weight_down(b, m).start())

    def arrive(n, m):
        b = order[n]
        weight_copy(b, m, y, 0, y_dev).wait_recv()
        pass_on(b, m)
        weight_y(b, m).start()

    def weight_ready(n):
        for m in range(PIECES):
            weight_copy(order[n], m, 1 - y, 2, y_dev).wait_recv()

    middle = u == 1

    def arrive_early(n, m):
        pl.when(middle)(lambda: arrive(n + 1, m))
        pl.when(jnp.logical_not(middle))(lambda: arrive(n, m))

    def to_flat(d):
        at = pl.ds(pl.multiple_of(d * shard_rows, shard_rows), shard_rows)
        flat[at, :] = slots[d].astype(jnp.float32)[:shard_rows]

    slot_z = [None] + [send(slots.at[own], slots.at[own], z_devs[k]) for k in range(1, 4)]
    slot_x = [send(slots.at[own], slots.at[own], x_dev)]
    slot_core = [send(slots.at[own], slots.at[own], core_dev)]
    load_up.wait()
    u_x = send(up_all.at[o], up_all.at[o], x_dev)
    u_core = send(up_all.at[o], up_all.at[o], core_dev)
    for k in range(1, 4):
        slot_z[k].wait_recv()
        at = slots.at[o * 4 + z_from[k]]
        slot_x.append(send(at, at, x_dev))
        slot_core.append(send(at, at, core_dev))
    load_w.wait()
    for m in range(PIECES):
        pass_on(z, m)
    for k in range(4):
        to_flat(o * 4 + z_from[k])
    for k in range(4):
        slot_x[k].wait_recv()
        at = slots.at[o_x * 4 + z_from[k]]
        slot_core.append(send(at, at, core_dev))
    u_x.wait_recv()
    u_far = send(up_all.at[o_x], up_all.at[o_x], core_dev)
    for k in range(4):
        to_flat(o_x * 4 + z_from[k])
    for k in range(8):
        slot_core[k].wait_recv()
        to_flat((o_core if k < 4 else o_diag) * 4 + z_from[k % 4])

    per_up = value_width // LANES
    up_m = jnp.concatenate(
        [flat[pl.ds(down_rows + j, rank, stride=per_up), :] for j in range(per_up)], axis=1
    ).astype(jnp.bfloat16)
    per_row = width // LANES

    def down_part(first, count):
        rows = [flat[pl.ds(first + j, rank, stride=per_row), :] for j in range(count)]
        return jnp.concatenate(rows, axis=1).astype(jnp.bfloat16)

    u_core.wait_recv()
    u_far.wait_recv()
    u_rows = 4 * tokens
    rank_all = dot(up_all[...].reshape(u_rows, value_width), up_m, (1, 1)).astype(jnp.bfloat16)

    block_copies = []

    def block_cols(n):
        return pl.ds(pl.multiple_of((o * 4 + order[n]) * feats, feats), feats)

    def block_math(n):
        cols = block_cols(n)
        per_block = feats // LANES
        d_block = down_part((o * 4 + order[n]) * per_block, per_block)
        value = dot(up_all[...].reshape(u_rows, value_width), w_buf[order[n]], (1, 1))
        value += scale * dot(rank_all, d_block, (1, 0))
        blocks[n] = value.astype(jnp.bfloat16).reshape(4, tokens, feats)
        out_ref[:, cols] = blocks[n, o]

    def block_send(n):
        for to, device in ((o_x, x_dev), (o_diag, diag_dev), (o_core, core_dev)):
            block_copies.append(send(blocks.at[n, to], out_ref.at[:, block_cols(n)], device))

    block_math(0)
    block_send(0)
    arrive(1, 0)
    pl.when(middle)(lambda: arrive(2, 0))

    own_rank_t = jnp.transpose(dot(up_all[o], up_m, (1, 1))).astype(jnp.bfloat16)
    load_act.wait()

    def part(n, projected):
        cols = pl.ds(pl.multiple_of(n * CHUNK, CHUNK), CHUNK)
        a_part = act_ref[:, cols]
        g_part = scale * dot(own_rank_t, a_part, (1, 0))
        for j in range(CHUNK // LANES):
            at = pl.ds(n * (CHUNK // LANES) + j, rank, stride=per_row)
            grad[at, :] = g_part[:, j * LANES : (j + 1) * LANES]
        return projected + dot(a_part, down_part(n * (CHUNK // LANES), CHUNK // LANES), (1, 1))

    projected = lax.fori_loop(
        0, width // CHUNK, part, jnp.zeros((tokens, rank), jnp.float32)
    ).astype(jnp.bfloat16)
    g_up = scale * dot(projected, up_all[o], (0, 0))
    for j in range(per_up):
        grad[pl.ds(down_rows + j, rank, stride=per_up), :] = g_up[:, j * LANES : (j + 1) * LANES]

    quarter = 4 * shard_rows

    def grad_rows(at):
        return pl.ds(pl.multiple_of(at * quarter, quarter), quarter)

    g_core_far = send(grad.at[grad_rows(o_diag)], from_core.at[0], core_dev)
    g_core_own = send(grad.at[grad_rows(o_core)], from_core.at[1], core_dev)
    arrive(1, 1)
    pl.when(middle)(lambda: arrive(2, 1))
    g_core_far.wait_recv()
    half_sum[0] = grad[grad_rows(o_x), :] + from_core[0]
    g_x = send(half_sum.at[0], from_x, x_dev)
    arrive_early(2, 0)
    g_core_own.wait_recv()
    half_sum[1] = grad[grad_rows(o), :] + from_core[1]
    arrive_early(2, 1)
    weight_ready(1)
    block_math(1)
    pl.when(jnp.logical_not(middle))(lambda: arrive(3, 0))
    weight_ready(2)
    block_math(2)
    pl.when(jnp.logical_not(middle))(lambda: arrive(3, 1))
    g_x.wait_recv()
    half_sum[1] += from_x[...]

    def shard(at):
        return pl.ds(pl.multiple_of(at * shard_rows, shard_rows), shard_rows)

    g_z = [
        send(half_sum.at[1, shard(z_to[k])], from_z.at[k - 1], z_devs[k]) for k in range(1, 4)
    ]
    block_send(1)
    block_send(2)
    weight_ready(3)
    block_math(3)
    block_send(3)
    for copy in g_z:
        copy.wait_recv()
    total = half_sum[1, shard(z), :] + from_z[0] + from_z[1] + from_z[2]
    clipped_ref[...] = total
    sq_own[...] = jnp.sum((total * total).reshape(shard_rows // 8, 8, LANES), axis=0)
    s_z = [send(sq_own, sq_z.at[k - 1], z_devs[k]) for k in range(1, 4)]
    for copy in s_z:
        copy.wait_recv()
    sq_line[...] = sq_own[...] + sq_z[0] + sq_z[1] + sq_z[2]
    s_s = [
        send(sq_line, sq_s.at[n], device)
        for n, device in enumerate((core_dev, x_dev, diag_dev))
    ]
    for copy in s_s:
        copy.wait_recv()
    sum_squares = jnp.sum(sq_line[...] + sq_s[0] + sq_s[1] + sq_s[2], keepdims=True)
    norm = jnp.sqrt(sum_squares + 1e-06)
    clipped_ref[...] = clipped_ref[...] * jnp.minimum(1.0, math.sqrt(params) / norm)
    for copy in block_copies:
        copy.wait_recv()
    for copy in used:
        copy.wait_send()
    for n in range(4):
        for m in range(PIECES):
            b = order[n]
            pl.when(goes_up(b))(lambda b=b, m=m: weight_up(b, m).wait_send())
            pl.when(goes_down(b))(lambda b=b, m=m: weight_down(b, m).wait_send())
            if n > 0:
                weight_y(b, m).wait_send()


def finish(
    rows_in,
    clipped_ref,
    master_ref,
    moment_ref,
    second_ref,
    rows_out,
    new_master_ref,
    new_moment_ref,
    new_second_ref,
    sem,
):
    step = rows_in.shape[0] // ROW_COPIES
    copies = []
    for n in range(ROW_COPIES):
        at = pl.ds(n * step, step)
        copies.append(pltpu.make_async_copy(rows_in.at[at], rows_out.at[at], sem.at[n]))
        copies[-1].start()
    new_master_ref[...], new_moment_ref[...], new_second_ref[...] = adam(
        clipped_ref[...], master_ref[...], moment_ref[...], second_ref[...]
    )
    for copy in copies:
        copy.wait()


N_COPIES = 64


def fused(rank, activations, upstream, weight, master, moment, second_moment):
    tokens, width = activations.shape
    value_width = upstream.shape[1]
    feats = weight.shape[0]
    shard_rows = master.shape[0] // LANES
    flat_rows = 16 * shard_rows
    padded = -(-shard_rows // 16) * 16
    state = jax.ShapeDtypeStruct((shard_rows, LANES), jnp.float32)
    bf16, f32 = jnp.bfloat16, jnp.float32
    vmem = pl.BlockSpec(memory_space=pltpu.VMEM)
    hbm = pl.BlockSpec(memory_space=pltpu.HBM)
    rows, clipped = pl.pallas_call(
        functools.partial(kernel, rank),
        out_shape=(jax.ShapeDtypeStruct((tokens, width), bf16), state),
        in_specs=[hbm] * 4,
        out_specs=(vmem,) * 2,
        scratch_shapes=[
            pltpu.VMEM((tokens, width), bf16),
            pltpu.VMEM((shard_rows, LANES), f32),
            pltpu.VMEM((16, padded, LANES), bf16),
            pltpu.VMEM((flat_rows, LANES), f32),
            pltpu.VMEM((4, tokens, value_width), bf16),
            pltpu.VMEM((4, feats, value_width), bf16),
            pltpu.VMEM((flat_rows, LANES), f32),
            pltpu.VMEM((2, 4 * shard_rows, LANES), f32),
            pltpu.VMEM((2, 4 * shard_rows, LANES), f32),
            pltpu.VMEM((4 * shard_rows, LANES), f32),
            pltpu.VMEM((3, shard_rows, LANES), f32),
            pltpu.VMEM((8, LANES), f32),
            pltpu.VMEM((3, 8, LANES), f32),
            pltpu.VMEM((8, LANES), f32),
            pltpu.VMEM((3, 8, LANES), f32),
            pltpu.VMEM((4, 4, tokens, feats), bf16),
            pltpu.SemaphoreType.DMA((4,)),
            pltpu.SemaphoreType.DMA((N_COPIES,)),
            pltpu.SemaphoreType.DMA((N_COPIES,)),
            pltpu.SemaphoreType.DMA((3, PIECES, 4)),
            pltpu.SemaphoreType.DMA((2, PIECES, 4)),
        ],
        compiler_params=pltpu.CompilerParams(
            collective_id=0, has_side_effects=True, vmem_limit_bytes=VMEM_GRANT
        ),
        name="adapter_backward",
    )(activations, upstream, weight, master.reshape(shard_rows, LANES))
    result = pl.pallas_call(
        finish,
        out_shape=(jax.ShapeDtypeStruct((tokens, width), bf16), state, state, state),
        in_specs=[hbm] + [vmem] * 4,
        out_specs=(hbm,) + (vmem,) * 3,
        scratch_shapes=[pltpu.SemaphoreType.DMA((ROW_COPIES,))],
        compiler_params=pltpu.CompilerParams(vmem_limit_bytes=VMEM_GRANT),
        name="finish",
    )(
        rows,
        clipped,
        master.reshape(shard_rows, LANES),
        moment.reshape(shard_rows, LANES),
        second_moment.reshape(shard_rows, LANES),
    )
    return (result[0],) + tuple(r.reshape(-1) for r in result[1:])


def solution(mesh):
    sizes = dict(mesh.shape)
    square = sizes["groups"] == 2 and sizes["outer"] == 4 and sizes["inner"] == 4

    def body(activations, upstream, weight, master, moment, second_moment):
        width, value_width = activations.shape[1], upstream.shape[1]
        rank = master.shape[0] * sizes["outer"] * sizes["inner"] // (width + value_width)
        fits = (
            activations.shape[0] % (16 * ROW_COPIES) == 0
            and width % CHUNK == 0
            and value_width % LANES == 0
            and weight.shape[0] % 256 == 0
            and master.shape[0] % (8 * LANES) == 0
            and rank % 16 == 0
        )
        if square and fits:
            return fused(rank, activations, upstream, weight, master, moment, second_moment)
        return per_device(activations, upstream, weight, master, moment, second_moment)

    return jax.shard_map(
        body,
        mesh=mesh,
        in_specs=(
            P(("groups", "outer", "inner"), None),
            P(("groups", "outer", "inner"), None),
            P(("outer", "inner"), None),
            P(("groups", "outer", "inner")),
            P(("groups", "outer", "inner")),
            P(("groups", "outer", "inner")),
        ),
        out_specs=(
            P(("groups", "outer", "inner"), None),
            P(("groups", "outer", "inner")),
            P(("groups", "outer", "inner")),
            P(("groups", "outer", "inner")),
        ),
        check_vma=False,
    )
```

```python
import functools
import math

import jax
import jax.numpy as jnp
from jax import lax
from jax.experimental import pallas as pl
from jax.experimental.pallas import tpu as pltpu
from jax.sharding import PartitionSpec as P

MESH = pl.DeviceIdType.MESH
LANES = 128
CHUNK = 1024
PIECES = 2
ROW_COPIES = 4
VMEM_GRANT = 56 * 1024 * 1024


def per_device(activations, upstream, frozen_weight_matrix, master, moment, second_moment):
    width = activations.shape[1]
    value_width = upstream.shape[1]
    whole = lax.all_gather(master.astype(jnp.bfloat16), ("outer", "inner"), axis=0, tiled=True)
    rank_activations = whole.shape[0] // (width + value_width)
    adapter_scale_factor = 0.5 / math.sqrt(rank_activations * value_width)
    down_weight_transposed = whole[: rank_activations * width].reshape(rank_activations, width)
    up_m = whole[rank_activations * width :].reshape(rank_activations, value_width)
    rank_gradient = jnp.dot(upstream, up_m.T, preferred_element_type=jnp.float32).astype(
        jnp.bfloat16
    )
    projected_rows = jnp.dot(
        activations, down_weight_transposed.T, preferred_element_type=jnp.float32
    ).astype(jnp.bfloat16)
    down_weight_gradient = adapter_scale_factor * jnp.dot(
        rank_gradient.T, activations, preferred_element_type=jnp.float32
    )
    up_weight_gradient = adapter_scale_factor * jnp.dot(
        projected_rows.T, upstream, preferred_element_type=jnp.float32
    )
    flat_grad = jnp.concatenate([down_weight_gradient.reshape(-1), up_weight_gradient.reshape(-1)])
    grad_shard = lax.psum_scatter(flat_grad, ("outer", "inner"), scatter_dimension=0, tiled=True)
    sum_squares = lax.psum(jnp.sum(grad_shard * grad_shard), ("outer", "inner"))
    feat_rows = frozen_weight_matrix.shape[0]
    feat_start = lax.axis_index(("outer", "inner")) * feat_rows
    own_cols = lax.dynamic_slice_in_dim(down_weight_transposed, feat_start, feat_rows, 1)
    tok_piece = lax.all_gather(upstream, ("outer", "inner"), axis=0, tiled=True)
    rank_piece = jnp.dot(tok_piece, up_m.T, preferred_element_type=jnp.float32).astype(jnp.bfloat16)
    frozen_output = lax.dot_general(
        tok_piece,
        frozen_weight_matrix,
        (((1,), (1,)), ((), ())),
        preferred_element_type=jnp.float32,
    )
    feat_block = (
        frozen_output
        + adapter_scale_factor * jnp.dot(rank_piece, own_cols, preferred_element_type=jnp.float32)
    ).astype(jnp.bfloat16)
    n_outer = lax.axis_size("outer")
    n_inner = lax.axis_size("inner")
    tok_count = upstream.shape[0]
    reordered = (
        feat_block.reshape(n_outer, n_inner, tok_count, feat_rows)
        .transpose(1, 0, 2, 3)
        .reshape(n_inner * n_outer * tok_count, feat_rows)
    )
    input_gradient_rows = lax.all_to_all(
        lax.all_to_all(reordered, "inner", split_axis=0, concat_axis=1, tiled=True),
        "outer",
        split_axis=0,
        concat_axis=1,
        tiled=True,
    )
    norm = jnp.sqrt(sum_squares + 1e-06)
    clipped = grad_shard * jnp.minimum(1.0, math.sqrt(whole.shape[0]) / norm)
    return (input_gradient_rows,) + adam(clipped, master, moment, second_moment)


def adam(clipped, master, moment, second_moment):
    new_moment = 0.9 * moment + 0.1 * clipped
    new_second = 0.999 * second_moment + 0.001 * clipped * clipped
    corr_one = 1.0 - 0.9**10
    corr_two = 1.0 - 0.999**10
    new_master = master - 0.1 * (new_moment / corr_one) / (jnp.sqrt(new_second / corr_two) + 1e-08)
    return new_master, new_moment, new_second


def dot(a, b, contract):
    return lax.dot_general(
        a, b, (((contract[0],), (contract[1],)), ((), ())), preferred_element_type=jnp.float32
    )


def kernel(
    rank,
    act_hbm,
    up_hbm,
    w_hbm,
    master_hbm,
    out_ref,
    clipped_ref,
    act_ref,
    master_ref,
    slots,
    flat,
    up_all,
    w_buf,
    grad,
    from_core,
    half_sum,
    from_x,
    from_z,
    sq_own,
    sq_z,
    sq_line,
    sq_s,
    blocks,
    load_sem,
    send_sem,
    recv_sem,
    w_send_sem,
    w_recv_sem,
    shard_send_sem,
    shard_recv_sem,
):
    y = lax.axis_index("groups")
    o = lax.axis_index("outer")
    z = lax.axis_index("inner")
    x, c = o // 2, lax.rem(o, 2)
    o_core = 2 * x + (1 - c)
    o_x = 2 * (1 - x) + c
    o_diag = 2 * (1 - x) + (1 - c)
    core_dev, x_dev, diag_dev = {"outer": o_core}, {"outer": o_x}, {"outer": o_diag}
    y_dev = {"groups": 1 - y}
    z_to = [None] + [lax.rem(z + k, 4) for k in range(1, 4)]
    z_from = [z] + [lax.rem(z + 4 - k, 4) for k in range(1, 4)]
    z_devs = [None] + [{"inner": z_to[k]} for k in range(1, 4)]
    high = z // 2
    u = z + high * (3 - 2 * z)
    order = [z] + [f + high * (3 - 2 * f) for f in (1 - u, 2, 3)]

    tokens, width = act_ref.shape
    value_width = up_all.shape[2]
    feats = w_buf.shape[1]
    half = feats // 2
    shard_rows = master_ref.shape[0]
    down_rows = rank * width // LANES
    params = 16 * shard_rows * LANES
    scale = 0.5 / math.sqrt(rank * value_width)

    barrier = pltpu.get_barrier_semaphore()
    partners = [core_dev, x_dev, diag_dev, y_dev] + z_devs[1:]
    for device in partners:
        pl.semaphore_signal(barrier, inc=1, device_id=device, device_id_type=MESH)

    loads = [
        pltpu.make_async_copy(src, dst, load_sem.at[n])
        for n, (src, dst) in enumerate(
            (
                (master_hbm, master_ref),
                (up_hbm, up_all.at[o]),
                (w_hbm, w_buf.at[z]),
                (act_hbm, act_ref),
            )
        )
    ]
    for load in loads:
        load.start()
    load_master, load_up, load_w, load_act = loads

    used = []

    def send(src, dst, device):
        at = len(used)
        copy = pltpu.make_async_remote_copy(
            src_ref=src,
            dst_ref=dst,
            send_sem=send_sem.at[at],
            recv_sem=recv_sem.at[at],
            device_id=device,
            device_id_type=MESH,
        )
        used.append(copy)
        copy.start()
        return copy

    own = o * 4 + z
    pad = slots.shape[1] - shard_rows
    load_master.wait()
    slots[own] = jnp.concatenate(
        [master_ref[...], jnp.zeros((pad, LANES), jnp.float32)], axis=0
    ).astype(jnp.bfloat16)
    pl.semaphore_wait(barrier, len(partners))

    piece = half // PIECES

    def weight_rows(part_y, m):
        return pl.ds(pl.multiple_of(part_y * half + m * piece, piece), piece)

    def weight_copy(b, m, part_y, way, device):
        at = w_buf.at[b, weight_rows(part_y, m)]
        return pltpu.make_async_remote_copy(
            src_ref=at,
            dst_ref=at,
            send_sem=w_send_sem.at[way, m, b],
            recv_sem=w_recv_sem.at[way // 2, m, b],
            device_id=device,
            device_id_type=MESH,
        )

    def weight_up(b, m):
        return weight_copy(b, m, y, 0, {"inner": z + 1})

    def weight_down(b, m):
        return weight_copy(b, m, y, 1, {"inner": z - 1})

    def weight_y(b, m):
        return weight_copy(b, m, y, 2, y_dev)

    goes_up = lambda b: (b <= z) & (z < 3)
    goes_down = lambda b: (b >= z) & (z > 0)

    def pass_on(b, m):
        pl.when(goes_up(b))(lambda: weight_up(b, m).start())
        pl.when(goes_down(b))(lambda: weight_down(b, m).start())

    def arrive(n, m):
        b = order[n]
        weight_copy(b, m, y, 0, y_dev).wait_recv()
        pass_on(b, m)
        weight_y(b, m).start()

    def weight_ready(n):
        for m in range(PIECES):
            weight_copy(order[n], m, 1 - y, 2, y_dev).wait_recv()

    middle = u == 1

    def arrive_early(n, m):
        pl.when(middle)(lambda: arrive(n + 1, m))
        pl.when(jnp.logical_not(middle))(lambda: arrive(n, m))

    def to_flat(d):
        at = pl.ds(pl.multiple_of(d * shard_rows, shard_rows), shard_rows)
        flat[at, :] = slots[d].astype(jnp.float32)[:shard_rows]

    slot_z = [None] + [send(slots.at[own], slots.at[own], z_devs[k]) for k in range(1, 4)]
    slot_x = [send(slots.at[own], slots.at[own], x_dev)]
    slot_core = [send(slots.at[own], slots.at[own], core_dev)]
    load_up.wait()
    u_x = send(up_all.at[o], up_all.at[o], x_dev)
    u_core = send(up_all.at[o], up_all.at[o], core_dev)
    for k in range(1, 4):
        slot_z[k].wait_recv()
        at = slots.at[o * 4 + z_from[k]]
        slot_x.append(send(at, at, x_dev))
        slot_core.append(send(at, at, core_dev))
    load_w.wait()
    for m in range(PIECES):
        pass_on(z, m)
    for k in range(4):
        to_flat(o * 4 + z_from[k])
    for k in range(4):
        slot_x[k].wait_recv()
        at = slots.at[o_x * 4 + z_from[k]]
        slot_core.append(send(at, at, core_dev))
    u_x.wait_recv()
    u_far = send(up_all.at[o_x], up_all.at[o_x], core_dev)
    for k in range(4):
        to_flat(o_x * 4 + z_from[k])
    for k in range(8):
        slot_core[k].wait_recv()
        to_flat((o_core if k < 4 else o_diag) * 4 + z_from[k % 4])

    per_up = value_width // LANES
    up_m = jnp.concatenate(
        [flat[pl.ds(down_rows + j, rank, stride=per_up), :] for j in range(per_up)], axis=1
    ).astype(jnp.bfloat16)
    per_row = width // LANES

    def down_part(first, count):
        rows = [flat[pl.ds(first + j, rank, stride=per_row), :] for j in range(count)]
        return jnp.concatenate(rows, axis=1).astype(jnp.bfloat16)

    u_core.wait_recv()
    u_far.wait_recv()
    u_rows = 4 * tokens
    rank_all = dot(up_all[...].reshape(u_rows, value_width), up_m, (1, 1)).astype(jnp.bfloat16)

    block_copies = []

    def block_cols(n):
        return pl.ds(pl.multiple_of((o * 4 + order[n]) * feats, feats), feats)

    def block_math(n):
        cols = block_cols(n)
        per_block = feats // LANES
        d_block = down_part((o * 4 + order[n]) * per_block, per_block)
        value = dot(up_all[...].reshape(u_rows, value_width), w_buf[order[n]], (1, 1))
        value += scale * dot(rank_all, d_block, (1, 0))
        blocks[n] = value.astype(jnp.bfloat16).reshape(4, tokens, feats)
        out_ref[:, cols] = blocks[n, o]

    def block_send(n):
        for to, device in ((o_x, x_dev), (o_diag, diag_dev), (o_core, core_dev)):
            block_copies.append(send(blocks.at[n, to], out_ref.at[:, block_cols(n)], device))

    block_math(0)
    block_send(0)
    arrive(1, 0)
    pl.when(middle)(lambda: arrive(2, 0))

    own_rank_t = jnp.transpose(dot(up_all[o], up_m, (1, 1))).astype(jnp.bfloat16)
    load_act.wait()

    def part(n, projected):
        cols = pl.ds(pl.multiple_of(n * CHUNK, CHUNK), CHUNK)
        a_part = act_ref[:, cols]
        g_part = scale * dot(own_rank_t, a_part, (1, 0))
        for j in range(CHUNK // LANES):
            at = pl.ds(n * (CHUNK // LANES) + j, rank, stride=per_row)
            grad[at, :] = g_part[:, j * LANES : (j + 1) * LANES]
        return projected + dot(a_part, down_part(n * (CHUNK // LANES), CHUNK // LANES), (1, 1))

    projected = lax.fori_loop(
        0, width // CHUNK, part, jnp.zeros((tokens, rank), jnp.float32)
    ).astype(jnp.bfloat16)
    arrive(1, 1)
    pl.when(middle)(lambda: arrive(2, 1))
    g_up = scale * dot(projected, up_all[o], (0, 0))
    for j in range(per_up):
        grad[pl.ds(down_rows + j, rank, stride=per_up), :] = g_up[:, j * LANES : (j + 1) * LANES]

    part_rows = 2 * shard_rows
    parts = [pl.ds(p * part_rows, part_rows) for p in range(2)]

    def grad_rows(at, p):
        return pl.ds(pl.multiple_of((2 * at + p) * part_rows, part_rows), part_rows)

    g_core_far = [
        send(grad.at[grad_rows(o_diag, p)], from_core.at[0, parts[p]], core_dev) for p in range(2)
    ]
    g_core_own = [
        send(grad.at[grad_rows(o_core, p)], from_core.at[1, parts[p]], core_dev) for p in range(2)
    ]
    weight_ready(1)
    block_math(1)
    block_send(1)
    g_x = []
    for p in range(2):
        g_core_far[p].wait_recv()
        half_sum[0, parts[p]] = grad[grad_rows(o_x, p), :] + from_core[0, parts[p]]
        g_x.append(send(half_sum.at[0, parts[p]], from_x.at[parts[p]], x_dev))
    arrive_early(2, 0)
    for p in range(2):
        g_core_own[p].wait_recv()
        half_sum[1, parts[p]] = grad[grad_rows(o, p), :] + from_core[1, parts[p]]
    arrive_early(2, 1)
    weight_ready(2)
    block_math(2)
    pl.when(jnp.logical_not(middle))(lambda: arrive(3, 0))
    pl.when(jnp.logical_not(middle))(lambda: arrive(3, 1))

    def shard(at):
        return pl.ds(pl.multiple_of(at * shard_rows, shard_rows), shard_rows)

    def shard_copy(to, source):
        return pltpu.make_async_remote_copy(
            src_ref=half_sum.at[1, shard(to)],
            dst_ref=from_z.at[source],
            send_sem=shard_send_sem.at[to],
            recv_sem=shard_recv_sem.at[source],
            device_id={"inner": to},
            device_id_type=MESH,
        )

    for p in range(2):
        g_x[p].wait_recv()
        half_sum[1, parts[p]] += from_x[parts[p]]
        for to in (2 * p, 2 * p + 1):
            pl.when(z != to)(lambda to=to: shard_copy(to, z).start())
    block_send(2)
    weight_ready(3)
    block_math(3)
    block_send(3)
    for k in range(1, 4):
        shard_copy(z_to[k], z_from[k]).wait_recv()
    total = half_sum[1, shard(z), :]
    for k in range(1, 4):
        total += from_z[z_from[k]]
    clipped_ref[...] = total
    sq_own[...] = jnp.sum((total * total).reshape(shard_rows // 8, 8, LANES), axis=0)
    s_z = [send(sq_own, sq_z.at[k - 1], z_devs[k]) for k in range(1, 4)]
    for copy in s_z:
        copy.wait_recv()
    sq_line[...] = sq_own[...] + sq_z[0] + sq_z[1] + sq_z[2]
    s_s = [
        send(sq_line, sq_s.at[n], device)
        for n, device in enumerate((core_dev, x_dev, diag_dev))
    ]
    for copy in s_s:
        copy.wait_recv()
    sum_squares = jnp.sum(sq_line[...] + sq_s[0] + sq_s[1] + sq_s[2], keepdims=True)
    norm = jnp.sqrt(sum_squares + 1e-06)
    clipped_ref[...] = clipped_ref[...] * jnp.minimum(1.0, math.sqrt(params) / norm)
    for copy in block_copies:
        copy.wait_recv()
    for copy in used:
        copy.wait_send()
    for k in range(1, 4):
        shard_copy(z_to[k], z).wait_send()
    for n in range(4):
        for m in range(PIECES):
            b = order[n]
            pl.when(goes_up(b))(lambda b=b, m=m: weight_up(b, m).wait_send())
            pl.when(goes_down(b))(lambda b=b, m=m: weight_down(b, m).wait_send())
            if n > 0:
                weight_y(b, m).wait_send()


def finish(
    rows_in,
    clipped_ref,
    master_ref,
    moment_ref,
    second_ref,
    rows_out,
    new_master_ref,
    new_moment_ref,
    new_second_ref,
    held,
    in_sem,
    out_sem,
):
    step = rows_in.shape[0] // ROW_COPIES
    cuts = [pl.ds(n * step, step) for n in range(ROW_COPIES)]
    fetch = [
        pltpu.make_async_copy(rows_in.at[at], held.at[at], in_sem.at[n])
        for n, at in enumerate(cuts)
    ]
    put = [
        pltpu.make_async_copy(held.at[at], rows_out.at[at], out_sem.at[n])
        for n, at in enumerate(cuts)
    ]
    for copy in fetch:
        copy.start()
    for n in range(ROW_COPIES):
        fetch[n].wait()
        put[n].start()
    new_master_ref[...], new_moment_ref[...], new_second_ref[...] = adam(
        clipped_ref[...], master_ref[...], moment_ref[...], second_ref[...]
    )
    for copy in put:
        copy.wait()


N_COPIES = 64


def fused(rank, activations, upstream, weight, master, moment, second_moment):
    tokens, width = activations.shape
    value_width = upstream.shape[1]
    feats = weight.shape[0]
    shard_rows = master.shape[0] // LANES
    flat_rows = 16 * shard_rows
    padded = -(-shard_rows // 16) * 16
    state = jax.ShapeDtypeStruct((shard_rows, LANES), jnp.float32)
    bf16, f32 = jnp.bfloat16, jnp.float32
    vmem = pl.BlockSpec(memory_space=pltpu.VMEM)
    hbm = pl.BlockSpec(memory_space=pltpu.HBM)
    rows, clipped = pl.pallas_call(
        functools.partial(kernel, rank),
        out_shape=(jax.ShapeDtypeStruct((tokens, width), bf16), state),
        in_specs=[hbm] * 4,
        out_specs=(vmem,) * 2,
        scratch_shapes=[
            pltpu.VMEM((tokens, width), bf16),
            pltpu.VMEM((shard_rows, LANES), f32),
            pltpu.VMEM((16, padded, LANES), bf16),
            pltpu.VMEM((flat_rows, LANES), f32),
            pltpu.VMEM((4, tokens, value_width), bf16),
            pltpu.VMEM((4, feats, value_width), bf16),
            pltpu.VMEM((flat_rows, LANES), f32),
            pltpu.VMEM((2, 4 * shard_rows, LANES), f32),
            pltpu.VMEM((2, 4 * shard_rows, LANES), f32),
            pltpu.VMEM((4 * shard_rows, LANES), f32),
            pltpu.VMEM((4, shard_rows, LANES), f32),
            pltpu.VMEM((8, LANES), f32),
            pltpu.VMEM((3, 8, LANES), f32),
            pltpu.VMEM((8, LANES), f32),
            pltpu.VMEM((3, 8, LANES), f32),
            pltpu.VMEM((4, 4, tokens, feats), bf16),
            pltpu.SemaphoreType.DMA((4,)),
            pltpu.SemaphoreType.DMA((N_COPIES,)),
            pltpu.SemaphoreType.DMA((N_COPIES,)),
            pltpu.SemaphoreType.DMA((3, PIECES, 4)),
            pltpu.SemaphoreType.DMA((2, PIECES, 4)),
            pltpu.SemaphoreType.DMA((4,)),
            pltpu.SemaphoreType.DMA((4,)),
        ],
        compiler_params=pltpu.CompilerParams(
            collective_id=0, has_side_effects=True, vmem_limit_bytes=VMEM_GRANT
        ),
        name="adapter_backward",
    )(activations, upstream, weight, master.reshape(shard_rows, LANES))
    result = pl.pallas_call(
        finish,
        out_shape=(jax.ShapeDtypeStruct((tokens, width), bf16), state, state, state),
        in_specs=[hbm] + [vmem] * 4,
        out_specs=(hbm,) + (vmem,) * 3,
        scratch_shapes=[
            pltpu.VMEM((tokens, width), bf16),
            pltpu.SemaphoreType.DMA((ROW_COPIES,)),
            pltpu.SemaphoreType.DMA((ROW_COPIES,)),
        ],
        compiler_params=pltpu.CompilerParams(vmem_limit_bytes=VMEM_GRANT),
        name="finish",
    )(
        rows,
        clipped,
        master.reshape(shard_rows, LANES),
        moment.reshape(shard_rows, LANES),
        second_moment.reshape(shard_rows, LANES),
    )
    return (result[0],) + tuple(r.reshape(-1) for r in result[1:])


def solution(mesh):
    sizes = dict(mesh.shape)
    square = sizes["groups"] == 2 and sizes["outer"] == 4 and sizes["inner"] == 4

    def body(activations, upstream, weight, master, moment, second_moment):
        width, value_width = activations.shape[1], upstream.shape[1]
        rank = master.shape[0] * sizes["outer"] * sizes["inner"] // (width + value_width)
        fits = (
            activations.shape[0] % (16 * ROW_COPIES) == 0
            and width % CHUNK == 0
            and value_width % LANES == 0
            and weight.shape[0] % 256 == 0
            and master.shape[0] % (8 * LANES) == 0
            and rank % 16 == 0
        )
        if square and fits:
            return fused(rank, activations, upstream, weight, master, moment, second_moment)
        return per_device(activations, upstream, weight, master, moment, second_moment)

    return jax.shard_map(
        body,
        mesh=mesh,
        in_specs=(
            P(("groups", "outer", "inner"), None),
            P(("groups", "outer", "inner"), None),
            P(("outer", "inner"), None),
            P(("groups", "outer", "inner")),
            P(("groups", "outer", "inner")),
            P(("groups", "outer", "inner")),
        ),
        out_specs=(
            P(("groups", "outer", "inner"), None),
            P(("groups", "outer", "inner")),
            P(("groups", "outer", "inner")),
            P(("groups", "outer", "inner")),
        ),
        check_vma=False,
    )
```

```python
import functools
import math

import jax
import jax.numpy as jnp
from jax import lax
from jax.experimental import pallas as pl
from jax.experimental.pallas import tpu as pltpu
from jax.sharding import PartitionSpec as P

MESH = pl.DeviceIdType.MESH
LANES = 128
CHUNK = 1024
PIECES = 2
ROW_COPIES = 4
VMEM_GRANT = 56 * 1024 * 1024


def per_device(activations, upstream, frozen_weight_matrix, master, moment, second_moment):
    width = activations.shape[1]
    value_width = upstream.shape[1]
    whole = lax.all_gather(master.astype(jnp.bfloat16), ("outer", "inner"), axis=0, tiled=True)
    rank_activations = whole.shape[0] // (width + value_width)
    adapter_scale_factor = 0.5 / math.sqrt(rank_activations * value_width)
    down_weight_transposed = whole[: rank_activations * width].reshape(rank_activations, width)
    up_m = whole[rank_activations * width :].reshape(rank_activations, value_width)
    rank_gradient = jnp.dot(upstream, up_m.T, preferred_element_type=jnp.float32).astype(
        jnp.bfloat16
    )
    projected_rows = jnp.dot(
        activations, down_weight_transposed.T, preferred_element_type=jnp.float32
    ).astype(jnp.bfloat16)
    down_weight_gradient = adapter_scale_factor * jnp.dot(
        rank_gradient.T, activations, preferred_element_type=jnp.float32
    )
    up_weight_gradient = adapter_scale_factor * jnp.dot(
        projected_rows.T, upstream, preferred_element_type=jnp.float32
    )
    flat_grad = jnp.concatenate([down_weight_gradient.reshape(-1), up_weight_gradient.reshape(-1)])
    grad_shard = lax.psum_scatter(flat_grad, ("outer", "inner"), scatter_dimension=0, tiled=True)
    sum_squares = lax.psum(jnp.sum(grad_shard * grad_shard), ("outer", "inner"))
    feat_rows = frozen_weight_matrix.shape[0]
    feat_start = lax.axis_index(("outer", "inner")) * feat_rows
    own_cols = lax.dynamic_slice_in_dim(down_weight_transposed, feat_start, feat_rows, 1)
    tok_piece = lax.all_gather(upstream, ("outer", "inner"), axis=0, tiled=True)
    rank_piece = jnp.dot(tok_piece, up_m.T, preferred_element_type=jnp.float32).astype(jnp.bfloat16)
    frozen_output = lax.dot_general(
        tok_piece,
        frozen_weight_matrix,
        (((1,), (1,)), ((), ())),
        preferred_element_type=jnp.float32,
    )
    feat_block = (
        frozen_output
        + adapter_scale_factor * jnp.dot(rank_piece, own_cols, preferred_element_type=jnp.float32)
    ).astype(jnp.bfloat16)
    n_outer = lax.axis_size("outer")
    n_inner = lax.axis_size("inner")
    tok_count = upstream.shape[0]
    reordered = (
        feat_block.reshape(n_outer, n_inner, tok_count, feat_rows)
        .transpose(1, 0, 2, 3)
        .reshape(n_inner * n_outer * tok_count, feat_rows)
    )
    input_gradient_rows = lax.all_to_all(
        lax.all_to_all(reordered, "inner", split_axis=0, concat_axis=1, tiled=True),
        "outer",
        split_axis=0,
        concat_axis=1,
        tiled=True,
    )
    norm = jnp.sqrt(sum_squares + 1e-06)
    clipped = grad_shard * jnp.minimum(1.0, math.sqrt(whole.shape[0]) / norm)
    return (input_gradient_rows,) + adam(clipped, master, moment, second_moment)


def adam(clipped, master, moment, second_moment):
    new_moment = 0.9 * moment + 0.1 * clipped
    new_second = 0.999 * second_moment + 0.001 * clipped * clipped
    corr_one = 1.0 - 0.9**10
    corr_two = 1.0 - 0.999**10
    new_master = master - 0.1 * (new_moment / corr_one) / (jnp.sqrt(new_second / corr_two) + 1e-08)
    return new_master, new_moment, new_second


def dot(a, b, contract):
    return lax.dot_general(
        a, b, (((contract[0],), (contract[1],)), ((), ())), preferred_element_type=jnp.float32
    )


def kernel(
    rank,
    act_hbm,
    up_hbm,
    w_hbm,
    master_hbm,
    out_ref,
    clipped_ref,
    act_ref,
    master_ref,
    slots,
    flat,
    up_all,
    w_buf,
    grad,
    from_core,
    half_sum,
    from_x,
    from_z,
    sq_own,
    sq_z,
    sq_line,
    sq_s,
    blocks,
    load_sem,
    send_sem,
    recv_sem,
    w_send_sem,
    w_recv_sem,
    shard_send_sem,
    shard_recv_sem,
):
    y = lax.axis_index("groups")
    o = lax.axis_index("outer")
    z = lax.axis_index("inner")
    x, c = o // 2, lax.rem(o, 2)
    o_core = 2 * x + (1 - c)
    o_x = 2 * (1 - x) + c
    o_diag = 2 * (1 - x) + (1 - c)
    core_dev, x_dev, diag_dev = {"outer": o_core}, {"outer": o_x}, {"outer": o_diag}
    y_dev = {"groups": 1 - y}
    z_to = [None] + [lax.rem(z + k, 4) for k in range(1, 4)]
    z_from = [z] + [lax.rem(z + 4 - k, 4) for k in range(1, 4)]
    z_devs = [None] + [{"inner": z_to[k]} for k in range(1, 4)]
    high = z // 2
    u = z + high * (3 - 2 * z)
    order = [z] + [f + high * (3 - 2 * f) for f in (1 - u, 2, 3)]

    tokens, width = act_ref.shape
    value_width = up_all.shape[2]
    feats = w_buf.shape[1]
    half = feats // 2
    shard_rows = master_ref.shape[0]
    down_rows = rank * width // LANES
    params = 16 * shard_rows * LANES
    scale = 0.5 / math.sqrt(rank * value_width)

    barrier = pltpu.get_barrier_semaphore()
    partners = [core_dev, x_dev, diag_dev, y_dev] + z_devs[1:]
    for device in partners:
        pl.semaphore_signal(barrier, inc=1, device_id=device, device_id_type=MESH)

    loads = [
        pltpu.make_async_copy(src, dst, load_sem.at[n])
        for n, (src, dst) in enumerate(
            (
                (master_hbm, master_ref),
                (up_hbm, up_all.at[o]),
                (w_hbm, w_buf.at[z]),
                (act_hbm, act_ref),
            )
        )
    ]
    for load in loads:
        load.start()
    load_master, load_up, load_w, load_act = loads

    used = []

    def send(src, dst, device):
        at = len(used)
        copy = pltpu.make_async_remote_copy(
            src_ref=src,
            dst_ref=dst,
            send_sem=send_sem.at[at],
            recv_sem=recv_sem.at[at],
            device_id=device,
            device_id_type=MESH,
        )
        used.append(copy)
        copy.start()
        return copy

    own = o * 4 + z
    pad = slots.shape[1] - shard_rows
    load_master.wait()
    slots[own] = jnp.concatenate(
        [master_ref[...], jnp.zeros((pad, LANES), jnp.float32)], axis=0
    ).astype(jnp.bfloat16)
    pl.semaphore_wait(barrier, len(partners))

    piece = half // PIECES

    def weight_rows(part_y, m):
        return pl.ds(pl.multiple_of(part_y * half + m * piece, piece), piece)

    def weight_copy(b, m, part_y, way, device):
        at = w_buf.at[b, weight_rows(part_y, m)]
        return pltpu.make_async_remote_copy(
            src_ref=at,
            dst_ref=at,
            send_sem=w_send_sem.at[way, m, b],
            recv_sem=w_recv_sem.at[way // 2, m, b],
            device_id=device,
            device_id_type=MESH,
        )

    def weight_up(b, m):
        return weight_copy(b, m, y, 0, {"inner": z + 1})

    def weight_down(b, m):
        return weight_copy(b, m, y, 1, {"inner": z - 1})

    def weight_y(b, m):
        return weight_copy(b, m, y, 2, y_dev)

    goes_up = lambda b: (b <= z) & (z < 3)
    goes_down = lambda b: (b >= z) & (z > 0)

    def pass_on(b, m):
        pl.when(goes_up(b))(lambda: weight_up(b, m).start())
        pl.when(goes_down(b))(lambda: weight_down(b, m).start())

    def arrive(n, m):
        b = order[n]
        weight_copy(b, m, y, 0, y_dev).wait_recv()
        pass_on(b, m)
        weight_y(b, m).start()

    def weight_ready(n):
        for m in range(PIECES):
            weight_copy(order[n], m, 1 - y, 2, y_dev).wait_recv()

    middle = u == 1

    def arrive_early(n, m):
        pl.when(middle)(lambda: arrive(n + 1, m))
        pl.when(jnp.logical_not(middle))(lambda: arrive(n, m))

    def to_flat(d):
        at = pl.ds(pl.multiple_of(d * shard_rows, shard_rows), shard_rows)
        flat[at, :] = slots[d].astype(jnp.float32)[:shard_rows]

    slot_z = [None] + [send(slots.at[own], slots.at[own], z_devs[k]) for k in range(1, 4)]
    slot_x = [send(slots.at[own], slots.at[own], x_dev)]
    slot_core = [send(slots.at[own], slots.at[own], core_dev)]
    load_up.wait()
    u_x = send(up_all.at[o], up_all.at[o], x_dev)
    u_core = send(up_all.at[o], up_all.at[o], core_dev)
    for k in range(1, 4):
        slot_z[k].wait_recv()
        at = slots.at[o * 4 + z_from[k]]
        slot_x.append(send(at, at, x_dev))
        slot_core.append(send(at, at, core_dev))
    load_w.wait()
    for m in range(PIECES):
        pass_on(z, m)
    for k in range(4):
        to_flat(o * 4 + z_from[k])
    for k in range(4):
        slot_x[k].wait_recv()
        at = slots.at[o_x * 4 + z_from[k]]
        slot_core.append(send(at, at, core_dev))
    u_x.wait_recv()
    u_far = send(up_all.at[o_x], up_all.at[o_x], core_dev)
    for k in range(4):
        to_flat(o_x * 4 + z_from[k])
    for k in range(8):
        slot_core[k].wait_recv()
        to_flat((o_core if k < 4 else o_diag) * 4 + z_from[k % 4])

    per_up = value_width // LANES
    up_m = jnp.concatenate(
        [flat[pl.ds(down_rows + j, rank, stride=per_up), :] for j in range(per_up)], axis=1
    ).astype(jnp.bfloat16)
    per_row = width // LANES

    def down_part(first, count):
        rows = [flat[pl.ds(first + j, rank, stride=per_row), :] for j in range(count)]
        return jnp.concatenate(rows, axis=1).astype(jnp.bfloat16)

    u_core.wait_recv()
    u_far.wait_recv()
    u_rows = 4 * tokens
    rank_all = dot(up_all[...].reshape(u_rows, value_width), up_m, (1, 1)).astype(jnp.bfloat16)

    block_copies = []

    def block_cols(n):
        return pl.ds(pl.multiple_of((o * 4 + order[n]) * feats, feats), feats)

    def block_math(n):
        cols = block_cols(n)
        per_block = feats // LANES
        d_block = down_part((o * 4 + order[n]) * per_block, per_block)
        value = dot(up_all[...].reshape(u_rows, value_width), w_buf[order[n]], (1, 1))
        value += scale * dot(rank_all, d_block, (1, 0))
        blocks[n] = value.astype(jnp.bfloat16).reshape(4, tokens, feats)
        out_ref[:, cols] = blocks[n, o]

    def block_send(n):
        for to, device in ((o_x, x_dev), (o_diag, diag_dev), (o_core, core_dev)):
            block_copies.append(send(blocks.at[n, to], out_ref.at[:, block_cols(n)], device))

    block_math(0)
    block_send(0)
    arrive(1, 0)
    pl.when(middle)(lambda: arrive(2, 0))

    own_rank_t = jnp.transpose(dot(up_all[o], up_m, (1, 1))).astype(jnp.bfloat16)
    load_act.wait()

    def part(n, projected):
        cols = pl.ds(pl.multiple_of(n * CHUNK, CHUNK), CHUNK)
        a_part = act_ref[:, cols]
        g_part = scale * dot(own_rank_t, a_part, (1, 0))
        for j in range(CHUNK // LANES):
            at = pl.ds(n * (CHUNK // LANES) + j, rank, stride=per_row)
            grad[at, :] = g_part[:, j * LANES : (j + 1) * LANES]
        return projected + dot(a_part, down_part(n * (CHUNK // LANES), CHUNK // LANES), (1, 1))

    projected = lax.fori_loop(
        0, width // CHUNK, part, jnp.zeros((tokens, rank), jnp.float32)
    ).astype(jnp.bfloat16)
    arrive(1, 1)
    pl.when(middle)(lambda: arrive(2, 1))
    g_up = scale * dot(projected, up_all[o], (0, 0))
    for j in range(per_up):
        grad[pl.ds(down_rows + j, rank, stride=per_up), :] = g_up[:, j * LANES : (j + 1) * LANES]

    part_rows = 2 * shard_rows
    parts = [pl.ds(p * part_rows, part_rows) for p in range(2)]

    def grad_rows(at, p):
        return pl.ds(pl.multiple_of((2 * at + p) * part_rows, part_rows), part_rows)

    g_core_far = [
        send(grad.at[grad_rows(o_diag, p)], from_core.at[0, parts[p]], core_dev) for p in range(2)
    ]
    g_core_own = [
        send(grad.at[grad_rows(o_core, p)], from_core.at[1, parts[p]], core_dev) for p in range(2)
    ]
    g_x = []
    for p in range(2):
        g_core_far[p].wait_recv()
        half_sum[0, parts[p]] = grad[grad_rows(o_x, p), :] + from_core[0, parts[p]]
        g_x.append(send(half_sum.at[0, parts[p]], from_x.at[parts[p]], x_dev))
    arrive_early(2, 0)
    for p in range(2):
        g_core_own[p].wait_recv()
        half_sum[1, parts[p]] = grad[grad_rows(o, p), :] + from_core[1, parts[p]]
    arrive_early(2, 1)
    weight_ready(1)
    block_math(1)

    def shard(at):
        return pl.ds(pl.multiple_of(at * shard_rows, shard_rows), shard_rows)

    def shard_copy(to, source):
        return pltpu.make_async_remote_copy(
            src_ref=half_sum.at[1, shard(to)],
            dst_ref=from_z.at[source],
            send_sem=shard_send_sem.at[to],
            recv_sem=shard_recv_sem.at[source],
            device_id={"inner": to},
            device_id_type=MESH,
        )

    for p in range(2):
        g_x[p].wait_recv()
        half_sum[1, parts[p]] += from_x[parts[p]]
        for to in (2 * p, 2 * p + 1):
            pl.when(z != to)(lambda to=to: shard_copy(to, z).start())
    block_send(1)
    pl.when(jnp.logical_not(middle))(lambda: arrive(3, 0))
    pl.when(jnp.logical_not(middle))(lambda: arrive(3, 1))
    weight_ready(2)
    block_math(2)
    block_send(2)
    for k in range(1, 4):
        shard_copy(z_to[k], z_from[k]).wait_recv()
    total = half_sum[1, shard(z), :]
    for k in range(1, 4):
        total += from_z[z_from[k]]
    clipped_ref[...] = total
    sq_own[...] = jnp.sum((total * total).reshape(shard_rows // 8, 8, LANES), axis=0)
    s_z = [send(sq_own, sq_z.at[k - 1], z_devs[k]) for k in range(1, 4)]
    weight_ready(3)
    block_math(3)
    block_send(3)
    for copy in s_z:
        copy.wait_recv()
    sq_line[...] = sq_own[...] + sq_z[0] + sq_z[1] + sq_z[2]
    s_s = [
        send(sq_line, sq_s.at[n], device)
        for n, device in enumerate((core_dev, x_dev, diag_dev))
    ]
    for copy in s_s:
        copy.wait_recv()
    sum_squares = jnp.sum(sq_line[...] + sq_s[0] + sq_s[1] + sq_s[2], keepdims=True)
    norm = jnp.sqrt(sum_squares + 1e-06)
    clipped_ref[...] = clipped_ref[...] * jnp.minimum(1.0, math.sqrt(params) / norm)
    for copy in block_copies:
        copy.wait_recv()
    for copy in used:
        copy.wait_send()
    for k in range(1, 4):
        shard_copy(z_to[k], z).wait_send()
    for n in range(4):
        for m in range(PIECES):
            b = order[n]
            pl.when(goes_up(b))(lambda b=b, m=m: weight_up(b, m).wait_send())
            pl.when(goes_down(b))(lambda b=b, m=m: weight_down(b, m).wait_send())
            if n > 0:
                weight_y(b, m).wait_send()


def finish(rows_in, *refs):
    states_in, rows_out, states_out = refs[:4], refs[4], refs[5:8]
    held, held_in, held_out, in_sem, out_sem = refs[8:]
    step = rows_in.shape[0] // ROW_COPIES
    cuts = [pl.ds(n * step, step) for n in range(ROW_COPIES)]
    moves = [(rows_in.at[at], held.at[at]) for at in cuts]
    moves += [(ref, held_in.at[n]) for n, ref in enumerate(states_in)]
    fetch = [pltpu.make_async_copy(a, b, in_sem.at[n]) for n, (a, b) in enumerate(moves)]
    moves = [(held.at[at], rows_out.at[at]) for at in cuts]
    moves += [(held_out.at[n], ref) for n, ref in enumerate(states_out)]
    put = [pltpu.make_async_copy(a, b, out_sem.at[n]) for n, (a, b) in enumerate(moves)]
    for copy in fetch:
        copy.start()
    for n in range(ROW_COPIES):
        fetch[n].wait()
        put[n].start()
    for copy in fetch[ROW_COPIES:]:
        copy.wait()
    held_out[0], held_out[1], held_out[2] = adam(*(held_in[n] for n in range(4)))
    for copy in put[ROW_COPIES:]:
        copy.start()
    for copy in put:
        copy.wait()


N_COPIES = 64


def fused(rank, activations, upstream, weight, master, moment, second_moment):
    tokens, width = activations.shape
    value_width = upstream.shape[1]
    feats = weight.shape[0]
    shard_rows = master.shape[0] // LANES
    flat_rows = 16 * shard_rows
    padded = -(-shard_rows // 16) * 16
    state = jax.ShapeDtypeStruct((shard_rows, LANES), jnp.float32)
    bf16, f32 = jnp.bfloat16, jnp.float32
    vmem = pl.BlockSpec(memory_space=pltpu.VMEM)
    hbm = pl.BlockSpec(memory_space=pltpu.HBM)
    rows, clipped = pl.pallas_call(
        functools.partial(kernel, rank),
        out_shape=(jax.ShapeDtypeStruct((tokens, width), bf16), state),
        in_specs=[hbm] * 4,
        out_specs=(vmem,) * 2,
        scratch_shapes=[
            pltpu.VMEM((tokens, width), bf16),
            pltpu.VMEM((shard_rows, LANES), f32),
            pltpu.VMEM((16, padded, LANES), bf16),
            pltpu.VMEM((flat_rows, LANES), f32),
            pltpu.VMEM((4, tokens, value_width), bf16),
            pltpu.VMEM((4, feats, value_width), bf16),
            pltpu.VMEM((flat_rows, LANES), f32),
            pltpu.VMEM((2, 4 * shard_rows, LANES), f32),
            pltpu.VMEM((2, 4 * shard_rows, LANES), f32),
            pltpu.VMEM((4 * shard_rows, LANES), f32),
            pltpu.VMEM((4, shard_rows, LANES), f32),
            pltpu.VMEM((8, LANES), f32),
            pltpu.VMEM((3, 8, LANES), f32),
            pltpu.VMEM((8, LANES), f32),
            pltpu.VMEM((3, 8, LANES), f32),
            pltpu.VMEM((4, 4, tokens, feats), bf16),
            pltpu.SemaphoreType.DMA((4,)),
            pltpu.SemaphoreType.DMA((N_COPIES,)),
            pltpu.SemaphoreType.DMA((N_COPIES,)),
            pltpu.SemaphoreType.DMA((3, PIECES, 4)),
            pltpu.SemaphoreType.DMA((2, PIECES, 4)),
            pltpu.SemaphoreType.DMA((4,)),
            pltpu.SemaphoreType.DMA((4,)),
        ],
        compiler_params=pltpu.CompilerParams(
            collective_id=0, has_side_effects=True, vmem_limit_bytes=VMEM_GRANT
        ),
        name="adapter_backward",
    )(activations, upstream, weight, master.reshape(shard_rows, LANES))
    result = pl.pallas_call(
        finish,
        out_shape=(jax.ShapeDtypeStruct((tokens, width), bf16), state, state, state),
        in_specs=[hbm] * 5,
        out_specs=(hbm,) * 4,
        scratch_shapes=[
            pltpu.VMEM((tokens, width), bf16),
            pltpu.VMEM((4, shard_rows, LANES), f32),
            pltpu.VMEM((3, shard_rows, LANES), f32),
            pltpu.SemaphoreType.DMA((ROW_COPIES + 4,)),
            pltpu.SemaphoreType.DMA((ROW_COPIES + 3,)),
        ],
        compiler_params=pltpu.CompilerParams(vmem_limit_bytes=VMEM_GRANT),
        name="finish",
    )(
        rows,
        clipped,
        master.reshape(shard_rows, LANES),
        moment.reshape(shard_rows, LANES),
        second_moment.reshape(shard_rows, LANES),
    )
    return (result[0],) + tuple(r.reshape(-1) for r in result[1:])


def solution(mesh):
    sizes = dict(mesh.shape)
    square = sizes["groups"] == 2 and sizes["outer"] == 4 and sizes["inner"] == 4

    def body(activations, upstream, weight, master, moment, second_moment):
        width, value_width = activations.shape[1], upstream.shape[1]
        rank = master.shape[0] * sizes["outer"] * sizes["inner"] // (width + value_width)
        fits = (
            activations.shape[0] % (16 * ROW_COPIES) == 0
            and width % CHUNK == 0
            and value_width % LANES == 0
            and weight.shape[0] % 256 == 0
            and master.shape[0] % (8 * LANES) == 0
            and rank % 16 == 0
        )
        if square and fits:
            return fused(rank, activations, upstream, weight, master, moment, second_moment)
        return per_device(activations, upstream, weight, master, moment, second_moment)

    return jax.shard_map(
        body,
        mesh=mesh,
        in_specs=(
            P(("groups", "outer", "inner"), None),
            P(("groups", "outer", "inner"), None),
            P(("outer", "inner"), None),
            P(("groups", "outer", "inner")),
            P(("groups", "outer", "inner")),
            P(("groups", "outer", "inner")),
        ),
        out_specs=(
            P(("groups", "outer", "inner"), None),
            P(("groups", "outer", "inner")),
            P(("groups", "outer", "inner")),
            P(("groups", "outer", "inner")),
        ),
        check_vma=False,
    )
```

```python
import functools
import math

import jax
import jax.numpy as jnp
from jax import lax
from jax.experimental import pallas as pl
from jax.experimental.pallas import tpu as pltpu
from jax.sharding import PartitionSpec as P

MESH = pl.DeviceIdType.MESH
LANES = 128
CHUNK = 1024
PIECES = 2
ROW_COPIES = 4
VMEM_GRANT = 56 * 1024 * 1024


def per_device(activations, upstream, frozen_weight_matrix, master, moment, second_moment):
    width = activations.shape[1]
    value_width = upstream.shape[1]
    whole = lax.all_gather(master.astype(jnp.bfloat16), ("outer", "inner"), axis=0, tiled=True)
    rank_activations = whole.shape[0] // (width + value_width)
    adapter_scale_factor = 0.5 / math.sqrt(rank_activations * value_width)
    down_weight_transposed = whole[: rank_activations * width].reshape(rank_activations, width)
    up_m = whole[rank_activations * width :].reshape(rank_activations, value_width)
    rank_gradient = jnp.dot(upstream, up_m.T, preferred_element_type=jnp.float32).astype(
        jnp.bfloat16
    )
    projected_rows = jnp.dot(
        activations, down_weight_transposed.T, preferred_element_type=jnp.float32
    ).astype(jnp.bfloat16)
    down_weight_gradient = adapter_scale_factor * jnp.dot(
        rank_gradient.T, activations, preferred_element_type=jnp.float32
    )
    up_weight_gradient = adapter_scale_factor * jnp.dot(
        projected_rows.T, upstream, preferred_element_type=jnp.float32
    )
    flat_grad = jnp.concatenate([down_weight_gradient.reshape(-1), up_weight_gradient.reshape(-1)])
    grad_shard = lax.psum_scatter(flat_grad, ("outer", "inner"), scatter_dimension=0, tiled=True)
    sum_squares = lax.psum(jnp.sum(grad_shard * grad_shard), ("outer", "inner"))
    feat_rows = frozen_weight_matrix.shape[0]
    feat_start = lax.axis_index(("outer", "inner")) * feat_rows
    own_cols = lax.dynamic_slice_in_dim(down_weight_transposed, feat_start, feat_rows, 1)
    tok_piece = lax.all_gather(upstream, ("outer", "inner"), axis=0, tiled=True)
    rank_piece = jnp.dot(tok_piece, up_m.T, preferred_element_type=jnp.float32).astype(jnp.bfloat16)
    frozen_output = lax.dot_general(
        tok_piece,
        frozen_weight_matrix,
        (((1,), (1,)), ((), ())),
        preferred_element_type=jnp.float32,
    )
    feat_block = (
        frozen_output
        + adapter_scale_factor * jnp.dot(rank_piece, own_cols, preferred_element_type=jnp.float32)
    ).astype(jnp.bfloat16)
    n_outer = lax.axis_size("outer")
    n_inner = lax.axis_size("inner")
    tok_count = upstream.shape[0]
    reordered = (
        feat_block.reshape(n_outer, n_inner, tok_count, feat_rows)
        .transpose(1, 0, 2, 3)
        .reshape(n_inner * n_outer * tok_count, feat_rows)
    )
    input_gradient_rows = lax.all_to_all(
        lax.all_to_all(reordered, "inner", split_axis=0, concat_axis=1, tiled=True),
        "outer",
        split_axis=0,
        concat_axis=1,
        tiled=True,
    )
    norm = jnp.sqrt(sum_squares + 1e-06)
    clipped = grad_shard * jnp.minimum(1.0, math.sqrt(whole.shape[0]) / norm)
    return (input_gradient_rows,) + adam(clipped, master, moment, second_moment)


def adam(clipped, master, moment, second_moment):
    new_moment = 0.9 * moment + 0.1 * clipped
    new_second = 0.999 * second_moment + 0.001 * clipped * clipped
    corr_one = 1.0 - 0.9**10
    corr_two = 1.0 - 0.999**10
    new_master = master - 0.1 * (new_moment / corr_one) / (jnp.sqrt(new_second / corr_two) + 1e-08)
    return new_master, new_moment, new_second


def dot(a, b, contract):
    return lax.dot_general(
        a, b, (((contract[0],), (contract[1],)), ((), ())), preferred_element_type=jnp.float32
    )


def kernel(
    rank,
    act_hbm,
    up_hbm,
    w_hbm,
    master_hbm,
    out_ref,
    clipped_ref,
    act_ref,
    master_ref,
    slots,
    flat,
    up_all,
    w_buf,
    grad,
    from_core,
    half_sum,
    from_x,
    from_z,
    sq_own,
    sq_z,
    sq_line,
    sq_s,
    blocks,
    load_sem,
    send_sem,
    recv_sem,
    w_send_sem,
    w_recv_sem,
    shard_send_sem,
    shard_recv_sem,
):
    y = lax.axis_index("groups")
    o = lax.axis_index("outer")
    z = lax.axis_index("inner")
    x, c = o // 2, lax.rem(o, 2)
    o_core = 2 * x + (1 - c)
    o_x = 2 * (1 - x) + c
    o_diag = 2 * (1 - x) + (1 - c)
    core_dev, x_dev, diag_dev = {"outer": o_core}, {"outer": o_x}, {"outer": o_diag}
    y_dev = {"groups": 1 - y}
    z_to = [None] + [lax.rem(z + k, 4) for k in range(1, 4)]
    z_from = [z] + [lax.rem(z + 4 - k, 4) for k in range(1, 4)]
    z_devs = [None] + [{"inner": z_to[k]} for k in range(1, 4)]
    high = z // 2
    u = z + high * (3 - 2 * z)
    order = [z] + [f + high * (3 - 2 * f) for f in (1 - u, 2, 3)]

    tokens, width = act_ref.shape
    value_width = up_all.shape[2]
    feats = w_buf.shape[1]
    half = feats // 2
    shard_rows = master_ref.shape[0]
    down_rows = rank * width // LANES
    params = 16 * shard_rows * LANES
    scale = 0.5 / math.sqrt(rank * value_width)

    barrier = pltpu.get_barrier_semaphore()
    partners = [core_dev, x_dev, diag_dev, y_dev] + z_devs[1:]
    for device in partners:
        pl.semaphore_signal(barrier, inc=1, device_id=device, device_id_type=MESH)

    loads = [
        pltpu.make_async_copy(src, dst, load_sem.at[n])
        for n, (src, dst) in enumerate(
            (
                (master_hbm, master_ref),
                (up_hbm, up_all.at[o]),
                (w_hbm, w_buf.at[z]),
                (act_hbm, act_ref),
            )
        )
    ]
    for load in loads:
        load.start()
    load_master, load_up, load_w, load_act = loads

    used = []

    def send(src, dst, device):
        at = len(used)
        copy = pltpu.make_async_remote_copy(
            src_ref=src,
            dst_ref=dst,
            send_sem=send_sem.at[at],
            recv_sem=recv_sem.at[at],
            device_id=device,
            device_id_type=MESH,
        )
        used.append(copy)
        copy.start()
        return copy

    own = o * 4 + z
    pad = slots.shape[1] - shard_rows
    load_master.wait()
    slots[own] = jnp.concatenate(
        [master_ref[...], jnp.zeros((pad, LANES), jnp.float32)], axis=0
    ).astype(jnp.bfloat16)
    pl.semaphore_wait(barrier, len(partners))

    piece = half // PIECES

    def weight_rows(part_y, m):
        return pl.ds(pl.multiple_of(part_y * half + m * piece, piece), piece)

    def weight_copy(b, m, part_y, way, device):
        at = w_buf.at[b, weight_rows(part_y, m)]
        return pltpu.make_async_remote_copy(
            src_ref=at,
            dst_ref=at,
            send_sem=w_send_sem.at[way, m, b],
            recv_sem=w_recv_sem.at[way // 2, m, b],
            device_id=device,
            device_id_type=MESH,
        )

    def weight_up(b, m):
        return weight_copy(b, m, y, 0, {"inner": z + 1})

    def weight_down(b, m):
        return weight_copy(b, m, y, 1, {"inner": z - 1})

    def weight_y(b, m):
        return weight_copy(b, m, y, 2, y_dev)

    goes_up = lambda b: (b <= z) & (z < 3)
    goes_down = lambda b: (b >= z) & (z > 0)

    def pass_on(b, m):
        pl.when(goes_up(b))(lambda: weight_up(b, m).start())
        pl.when(goes_down(b))(lambda: weight_down(b, m).start())

    def arrive(n, m):
        b = order[n]
        weight_copy(b, m, y, 0, y_dev).wait_recv()
        pass_on(b, m)
        weight_y(b, m).start()

    def weight_ready(n):
        for m in range(PIECES):
            weight_copy(order[n], m, 1 - y, 2, y_dev).wait_recv()

    middle = u == 1

    def arrive_early(n, m):
        pl.when(middle)(lambda: arrive(n + 1, m))
        pl.when(jnp.logical_not(middle))(lambda: arrive(n, m))

    def to_flat(d):
        at = pl.ds(pl.multiple_of(d * shard_rows, shard_rows), shard_rows)
        flat[at, :] = slots[d].astype(jnp.float32)[:shard_rows]

    slot_z = [None] + [send(slots.at[own], slots.at[own], z_devs[k]) for k in range(1, 4)]
    slot_x = [send(slots.at[own], slots.at[own], x_dev)]
    slot_core = [send(slots.at[own], slots.at[own], core_dev)]
    load_up.wait()
    u_x = send(up_all.at[o], up_all.at[o], x_dev)
    u_core = send(up_all.at[o], up_all.at[o], core_dev)
    for k in range(1, 4):
        slot_z[k].wait_recv()
        at = slots.at[o * 4 + z_from[k]]
        slot_x.append(send(at, at, x_dev))
        slot_core.append(send(at, at, core_dev))
    load_w.wait()
    for m in range(PIECES):
        pass_on(z, m)
    for k in range(4):
        to_flat(o * 4 + z_from[k])
    for k in range(4):
        slot_x[k].wait_recv()
        at = slots.at[o_x * 4 + z_from[k]]
        slot_core.append(send(at, at, core_dev))
    u_x.wait_recv()
    u_far = send(up_all.at[o_x], up_all.at[o_x], core_dev)
    for k in range(4):
        to_flat(o_x * 4 + z_from[k])
    for k in range(8):
        slot_core[k].wait_recv()
        to_flat((o_core if k < 4 else o_diag) * 4 + z_from[k % 4])

    per_up = value_width // LANES
    up_m = jnp.concatenate(
        [flat[pl.ds(down_rows + j, rank, stride=per_up), :] for j in range(per_up)], axis=1
    ).astype(jnp.bfloat16)
    per_row = width // LANES

    def down_part(first, count):
        rows = [flat[pl.ds(first + j, rank, stride=per_row), :] for j in range(count)]
        return jnp.concatenate(rows, axis=1).astype(jnp.bfloat16)

    u_core.wait_recv()
    u_far.wait_recv()
    u_rows = 4 * tokens
    rank_all = dot(up_all[...].reshape(u_rows, value_width), up_m, (1, 1)).astype(jnp.bfloat16)

    block_copies = []

    def block_cols(n, h):
        at = (o * 4 + order[n]) * 2 + (y if h == 0 else 1 - y)
        return pl.ds(pl.multiple_of(at * half, half), half)

    def block_math(n, h):
        side = y if h == 0 else 1 - y
        per_block = half // LANES
        d_block = down_part(((o * 4 + order[n]) * 2 + side) * per_block, per_block)
        w = w_buf[order[n], pl.ds(pl.multiple_of(side * half, half), half), :]
        value = dot(up_all[...].reshape(u_rows, value_width), w, (1, 1))
        value += scale * dot(rank_all, d_block, (1, 0))
        blocks[n, h] = value.astype(jnp.bfloat16).reshape(4, tokens, half)
        out_ref[:, block_cols(n, h)] = blocks[n, h, o]

    def block_send(n, h):
        for to, device in ((o_x, x_dev), (o_diag, diag_dev), (o_core, core_dev)):
            block_copies.append(
                send(blocks.at[n, h, to], out_ref.at[:, block_cols(n, h)], device)
            )

    def block(n, h):
        block_math(n, h)
        block_send(n, h)

    block(0, 0)
    block(0, 1)
    arrive(1, 0)
    pl.when(middle)(lambda: arrive(2, 0))

    own_rank_t = jnp.transpose(dot(up_all[o], up_m, (1, 1))).astype(jnp.bfloat16)
    load_act.wait()

    def part(n, projected):
        cols = pl.ds(pl.multiple_of(n * CHUNK, CHUNK), CHUNK)
        a_part = act_ref[:, cols]
        g_part = scale * dot(own_rank_t, a_part, (1, 0))
        for j in range(CHUNK // LANES):
            at = pl.ds(n * (CHUNK // LANES) + j, rank, stride=per_row)
            grad[at, :] = g_part[:, j * LANES : (j + 1) * LANES]
        return projected + dot(a_part, down_part(n * (CHUNK // LANES), CHUNK // LANES), (1, 1))

    projected = lax.fori_loop(
        0, width // CHUNK, part, jnp.zeros((tokens, rank), jnp.float32)
    ).astype(jnp.bfloat16)
    arrive(1, 1)
    pl.when(middle)(lambda: arrive(2, 1))
    g_up = scale * dot(projected, up_all[o], (0, 0))
    for j in range(per_up):
        grad[pl.ds(down_rows + j, rank, stride=per_up), :] = g_up[:, j * LANES : (j + 1) * LANES]

    part_rows = 2 * shard_rows
    parts = [pl.ds(p * part_rows, part_rows) for p in range(2)]

    def grad_rows(at, p):
        return pl.ds(pl.multiple_of((2 * at + p) * part_rows, part_rows), part_rows)

    g_core_far = [
        send(grad.at[grad_rows(o_diag, p)], from_core.at[0, parts[p]], core_dev) for p in range(2)
    ]
    g_core_own = [
        send(grad.at[grad_rows(o_core, p)], from_core.at[1, parts[p]], core_dev) for p in range(2)
    ]
    g_x = []
    for p in range(2):
        g_core_far[p].wait_recv()
        half_sum[0, parts[p]] = grad[grad_rows(o_x, p), :] + from_core[0, parts[p]]
        g_x.append(send(half_sum.at[0, parts[p]], from_x.at[parts[p]], x_dev))
    arrive_early(2, 0)
    for p in range(2):
        g_core_own[p].wait_recv()
        half_sum[1, parts[p]] = grad[grad_rows(o, p), :] + from_core[1, parts[p]]
    arrive_early(2, 1)
    block_math(1, 0)
    weight_ready(1)
    block_math(1, 1)

    def shard(at):
        return pl.ds(pl.multiple_of(at * shard_rows, shard_rows), shard_rows)

    def shard_copy(to, source):
        return pltpu.make_async_remote_copy(
            src_ref=half_sum.at[1, shard(to)],
            dst_ref=from_z.at[source],
            send_sem=shard_send_sem.at[to],
            recv_sem=shard_recv_sem.at[source],
            device_id={"inner": to},
            device_id_type=MESH,
        )

    for p in range(2):
        g_x[p].wait_recv()
        half_sum[1, parts[p]] += from_x[parts[p]]
        for to in (2 * p, 2 * p + 1):
            pl.when(z != to)(lambda to=to: shard_copy(to, z).start())
        if p == 0:
            pl.when(jnp.logical_not(middle))(lambda: arrive(3, 0))
    block_send(1, 0)
    block_send(1, 1)
    pl.when(jnp.logical_not(middle))(lambda: arrive(3, 1))
    block(2, 0)
    weight_ready(2)
    block(2, 1)
    block(3, 0)
    for k in range(1, 4):
        shard_copy(z_to[k], z_from[k]).wait_recv()
    total = half_sum[1, shard(z), :]
    for k in range(1, 4):
        total += from_z[z_from[k]]
    clipped_ref[...] = total
    sq_own[...] = jnp.sum((total * total).reshape(shard_rows // 8, 8, LANES), axis=0)
    s_z = [send(sq_own, sq_z.at[k - 1], z_devs[k]) for k in range(1, 4)]
    weight_ready(3)
    block(3, 1)
    for copy in s_z:
        copy.wait_recv()
    sq_line[...] = sq_own[...] + sq_z[0] + sq_z[1] + sq_z[2]
    s_s = [
        send(sq_line, sq_s.at[n], device)
        for n, device in enumerate((core_dev, x_dev, diag_dev))
    ]
    for copy in s_s:
        copy.wait_recv()
    sum_squares = jnp.sum(sq_line[...] + sq_s[0] + sq_s[1] + sq_s[2], keepdims=True)
    norm = jnp.sqrt(sum_squares + 1e-06)
    clipped_ref[...] = clipped_ref[...] * jnp.minimum(1.0, math.sqrt(params) / norm)
    for copy in block_copies:
        copy.wait_recv()
    for copy in used:
        copy.wait_send()
    for k in range(1, 4):
        shard_copy(z_to[k], z).wait_send()
    for n in range(4):
        for m in range(PIECES):
            b = order[n]
            pl.when(goes_up(b))(lambda b=b, m=m: weight_up(b, m).wait_send())
            pl.when(goes_down(b))(lambda b=b, m=m: weight_down(b, m).wait_send())
            if n > 0:
                weight_y(b, m).wait_send()


def finish(rows_in, *refs):
    states_in, rows_out, states_out = refs[:4], refs[4], refs[5:8]
    held, held_in, held_out, in_sem, out_sem = refs[8:]
    step = rows_in.shape[0] // ROW_COPIES
    cuts = [pl.ds(n * step, step) for n in range(ROW_COPIES)]
    moves = [(rows_in.at[at], held.at[at]) for at in cuts]
    moves += [(ref, held_in.at[n]) for n, ref in enumerate(states_in)]
    fetch = [pltpu.make_async_copy(a, b, in_sem.at[n]) for n, (a, b) in enumerate(moves)]
    moves = [(held.at[at], rows_out.at[at]) for at in cuts]
    moves += [(held_out.at[n], ref) for n, ref in enumerate(states_out)]
    put = [pltpu.make_async_copy(a, b, out_sem.at[n]) for n, (a, b) in enumerate(moves)]
    for copy in fetch:
        copy.start()
    for n in range(ROW_COPIES):
        fetch[n].wait()
        put[n].start()
    for copy in fetch[ROW_COPIES:]:
        copy.wait()
    held_out[0], held_out[1], held_out[2] = adam(*(held_in[n] for n in range(4)))
    for copy in put[ROW_COPIES:]:
        copy.start()
    for copy in put:
        copy.wait()


N_COPIES = 64


def fused(rank, activations, upstream, weight, master, moment, second_moment):
    tokens, width = activations.shape
    value_width = upstream.shape[1]
    feats = weight.shape[0]
    shard_rows = master.shape[0] // LANES
    flat_rows = 16 * shard_rows
    padded = -(-shard_rows // 16) * 16
    state = jax.ShapeDtypeStruct((shard_rows, LANES), jnp.float32)
    bf16, f32 = jnp.bfloat16, jnp.float32
    vmem = pl.BlockSpec(memory_space=pltpu.VMEM)
    hbm = pl.BlockSpec(memory_space=pltpu.HBM)
    rows, clipped = pl.pallas_call(
        functools.partial(kernel, rank),
        out_shape=(jax.ShapeDtypeStruct((tokens, width), bf16), state),
        in_specs=[hbm] * 4,
        out_specs=(vmem,) * 2,
        scratch_shapes=[
            pltpu.VMEM((tokens, width), bf16),
            pltpu.VMEM((shard_rows, LANES), f32),
            pltpu.VMEM((16, padded, LANES), bf16),
            pltpu.VMEM((flat_rows, LANES), f32),
            pltpu.VMEM((4, tokens, value_width), bf16),
            pltpu.VMEM((4, feats, value_width), bf16),
            pltpu.VMEM((flat_rows, LANES), f32),
            pltpu.VMEM((2, 4 * shard_rows, LANES), f32),
            pltpu.VMEM((2, 4 * shard_rows, LANES), f32),
            pltpu.VMEM((4 * shard_rows, LANES), f32),
            pltpu.VMEM((4, shard_rows, LANES), f32),
            pltpu.VMEM((8, LANES), f32),
            pltpu.VMEM((3, 8, LANES), f32),
            pltpu.VMEM((8, LANES), f32),
            pltpu.VMEM((3, 8, LANES), f32),
            pltpu.VMEM((4, 2, 4, tokens, feats // 2), bf16),
            pltpu.SemaphoreType.DMA((4,)),
            pltpu.SemaphoreType.DMA((N_COPIES,)),
            pltpu.SemaphoreType.DMA((N_COPIES,)),
            pltpu.SemaphoreType.DMA((3, PIECES, 4)),
            pltpu.SemaphoreType.DMA((2, PIECES, 4)),
            pltpu.SemaphoreType.DMA((4,)),
            pltpu.SemaphoreType.DMA((4,)),
        ],
        compiler_params=pltpu.CompilerParams(
            collective_id=0, has_side_effects=True, vmem_limit_bytes=VMEM_GRANT
        ),
        name="adapter_backward",
    )(activations, upstream, weight, master.reshape(shard_rows, LANES))
    result = pl.pallas_call(
        finish,
        out_shape=(jax.ShapeDtypeStruct((tokens, width), bf16), state, state, state),
        in_specs=[hbm] * 5,
        out_specs=(hbm,) * 4,
        scratch_shapes=[
            pltpu.VMEM((tokens, width), bf16),
            pltpu.VMEM((4, shard_rows, LANES), f32),
            pltpu.VMEM((3, shard_rows, LANES), f32),
            pltpu.SemaphoreType.DMA((ROW_COPIES + 4,)),
            pltpu.SemaphoreType.DMA((ROW_COPIES + 3,)),
        ],
        compiler_params=pltpu.CompilerParams(vmem_limit_bytes=VMEM_GRANT),
        name="finish",
    )(
        rows,
        clipped,
        master.reshape(shard_rows, LANES),
        moment.reshape(shard_rows, LANES),
        second_moment.reshape(shard_rows, LANES),
    )
    return (result[0],) + tuple(r.reshape(-1) for r in result[1:])


def solution(mesh):
    sizes = dict(mesh.shape)
    square = sizes["groups"] == 2 and sizes["outer"] == 4 and sizes["inner"] == 4

    def body(activations, upstream, weight, master, moment, second_moment):
        width, value_width = activations.shape[1], upstream.shape[1]
        rank = master.shape[0] * sizes["outer"] * sizes["inner"] // (width + value_width)
        fits = (
            activations.shape[0] % (16 * ROW_COPIES) == 0
            and width % CHUNK == 0
            and value_width % LANES == 0
            and weight.shape[0] % 256 == 0
            and master.shape[0] % (8 * LANES) == 0
            and rank % 16 == 0
        )
        if square and fits:
            return fused(rank, activations, upstream, weight, master, moment, second_moment)
        return per_device(activations, upstream, weight, master, moment, second_moment)

    return jax.shard_map(
        body,
        mesh=mesh,
        in_specs=(
            P(("groups", "outer", "inner"), None),
            P(("groups", "outer", "inner"), None),
            P(("outer", "inner"), None),
            P(("groups", "outer", "inner")),
            P(("groups", "outer", "inner")),
            P(("groups", "outer", "inner")),
        ),
        out_specs=(
            P(("groups", "outer", "inner"), None),
            P(("groups", "outer", "inner")),
            P(("groups", "outer", "inner")),
            P(("groups", "outer", "inner")),
        ),
        check_vma=False,
    )
```

```python
import functools
import math

import jax
import jax.numpy as jnp
from jax import lax
from jax.experimental import pallas as pl
from jax.experimental.pallas import tpu as pltpu
from jax.sharding import PartitionSpec as P

MESH = pl.DeviceIdType.MESH
LANES = 128
CHUNK = 1024
PIECES = 2
ROW_COPIES = 4
VMEM_GRANT = 56 * 1024 * 1024


def per_device(activations, upstream, frozen_weight_matrix, master, moment, second_moment):
    width = activations.shape[1]
    value_width = upstream.shape[1]
    whole = lax.all_gather(master.astype(jnp.bfloat16), ("outer", "inner"), axis=0, tiled=True)
    rank_activations = whole.shape[0] // (width + value_width)
    adapter_scale_factor = 0.5 / math.sqrt(rank_activations * value_width)
    down_weight_transposed = whole[: rank_activations * width].reshape(rank_activations, width)
    up_m = whole[rank_activations * width :].reshape(rank_activations, value_width)
    rank_gradient = jnp.dot(upstream, up_m.T, preferred_element_type=jnp.float32).astype(
        jnp.bfloat16
    )
    projected_rows = jnp.dot(
        activations, down_weight_transposed.T, preferred_element_type=jnp.float32
    ).astype(jnp.bfloat16)
    down_weight_gradient = adapter_scale_factor * jnp.dot(
        rank_gradient.T, activations, preferred_element_type=jnp.float32
    )
    up_weight_gradient = adapter_scale_factor * jnp.dot(
        projected_rows.T, upstream, preferred_element_type=jnp.float32
    )
    flat_grad = jnp.concatenate([down_weight_gradient.reshape(-1), up_weight_gradient.reshape(-1)])
    grad_shard = lax.psum_scatter(flat_grad, ("outer", "inner"), scatter_dimension=0, tiled=True)
    sum_squares = lax.psum(jnp.sum(grad_shard * grad_shard), ("outer", "inner"))
    feat_rows = frozen_weight_matrix.shape[0]
    feat_start = lax.axis_index(("outer", "inner")) * feat_rows
    own_cols = lax.dynamic_slice_in_dim(down_weight_transposed, feat_start, feat_rows, 1)
    tok_piece = lax.all_gather(upstream, ("outer", "inner"), axis=0, tiled=True)
    rank_piece = jnp.dot(tok_piece, up_m.T, preferred_element_type=jnp.float32).astype(jnp.bfloat16)
    frozen_output = lax.dot_general(
        tok_piece,
        frozen_weight_matrix,
        (((1,), (1,)), ((), ())),
        preferred_element_type=jnp.float32,
    )
    feat_block = (
        frozen_output
        + adapter_scale_factor * jnp.dot(rank_piece, own_cols, preferred_element_type=jnp.float32)
    ).astype(jnp.bfloat16)
    n_outer = lax.axis_size("outer")
    n_inner = lax.axis_size("inner")
    tok_count = upstream.shape[0]
    reordered = (
        feat_block.reshape(n_outer, n_inner, tok_count, feat_rows)
        .transpose(1, 0, 2, 3)
        .reshape(n_inner * n_outer * tok_count, feat_rows)
    )
    input_gradient_rows = lax.all_to_all(
        lax.all_to_all(reordered, "inner", split_axis=0, concat_axis=1, tiled=True),
        "outer",
        split_axis=0,
        concat_axis=1,
        tiled=True,
    )
    norm = jnp.sqrt(sum_squares + 1e-06)
    clipped = grad_shard * jnp.minimum(1.0, math.sqrt(whole.shape[0]) / norm)
    return (input_gradient_rows,) + adam(clipped, master, moment, second_moment)


def adam(clipped, master, moment, second_moment):
    new_moment = 0.9 * moment + 0.1 * clipped
    new_second = 0.999 * second_moment + 0.001 * clipped * clipped
    corr_one = 1.0 - 0.9**10
    corr_two = 1.0 - 0.999**10
    new_master = master - 0.1 * (new_moment / corr_one) / (jnp.sqrt(new_second / corr_two) + 1e-08)
    return new_master, new_moment, new_second


def dot(a, b, contract):
    return lax.dot_general(
        a, b, (((contract[0],), (contract[1],)), ((), ())), preferred_element_type=jnp.float32
    )


def kernel(
    rank,
    act_hbm,
    up_hbm,
    w_hbm,
    master_hbm,
    out_ref,
    clipped_ref,
    act_ref,
    master_ref,
    slots,
    flat,
    up_all,
    w_buf,
    grad,
    from_core,
    half_sum,
    from_x,
    from_z,
    sq_own,
    sq_z,
    sq_line,
    sq_s,
    blocks,
    load_sem,
    send_sem,
    recv_sem,
    w_send_sem,
    w_recv_sem,
    shard_send_sem,
    shard_recv_sem,
):
    y = lax.axis_index("groups")
    o = lax.axis_index("outer")
    z = lax.axis_index("inner")
    x, c = o // 2, lax.rem(o, 2)
    o_core = 2 * x + (1 - c)
    o_x = 2 * (1 - x) + c
    o_diag = 2 * (1 - x) + (1 - c)
    core_dev, x_dev, diag_dev = {"outer": o_core}, {"outer": o_x}, {"outer": o_diag}
    y_dev = {"groups": 1 - y}
    z_to = [None] + [lax.rem(z + k, 4) for k in range(1, 4)]
    z_from = [z] + [lax.rem(z + 4 - k, 4) for k in range(1, 4)]
    z_devs = [None] + [{"inner": z_to[k]} for k in range(1, 4)]
    high = z // 2
    u = z + high * (3 - 2 * z)
    order = [z] + [f + high * (3 - 2 * f) for f in (1 - u, 2, 3)]

    tokens, width = act_ref.shape
    value_width = up_all.shape[2]
    feats = w_buf.shape[1]
    half = feats // 2
    shard_rows = master_ref.shape[0]
    down_rows = rank * width // LANES
    params = 16 * shard_rows * LANES
    scale = 0.5 / math.sqrt(rank * value_width)

    barrier = pltpu.get_barrier_semaphore()
    partners = [core_dev, x_dev, diag_dev, y_dev] + z_devs[1:]
    for device in partners:
        pl.semaphore_signal(barrier, inc=1, device_id=device, device_id_type=MESH)

    loads = [
        pltpu.make_async_copy(src, dst, load_sem.at[n])
        for n, (src, dst) in enumerate(
            (
                (master_hbm, master_ref),
                (up_hbm, up_all.at[o]),
                (w_hbm, w_buf.at[z]),
                (act_hbm, act_ref),
            )
        )
    ]
    for load in loads:
        load.start()
    load_master, load_up, load_w, load_act = loads

    used = []

    def send(src, dst, device):
        at = len(used)
        copy = pltpu.make_async_remote_copy(
            src_ref=src,
            dst_ref=dst,
            send_sem=send_sem.at[at],
            recv_sem=recv_sem.at[at],
            device_id=device,
            device_id_type=MESH,
        )
        used.append(copy)
        copy.start()
        return copy

    own = o * 4 + z
    pad = slots.shape[1] - shard_rows
    load_master.wait()
    slots[own] = jnp.concatenate(
        [master_ref[...], jnp.zeros((pad, LANES), jnp.float32)], axis=0
    ).astype(jnp.bfloat16)
    pl.semaphore_wait(barrier, len(partners))

    piece = half // PIECES

    def weight_rows(part_y, m):
        return pl.ds(pl.multiple_of(part_y * half + m * piece, piece), piece)

    def weight_copy(b, m, part_y, way, device):
        at = w_buf.at[b, weight_rows(part_y, m)]
        return pltpu.make_async_remote_copy(
            src_ref=at,
            dst_ref=at,
            send_sem=w_send_sem.at[way, m, b],
            recv_sem=w_recv_sem.at[way // 2, m, b],
            device_id=device,
            device_id_type=MESH,
        )

    def weight_up(b, m):
        return weight_copy(b, m, y, 0, {"inner": z + 1})

    def weight_down(b, m):
        return weight_copy(b, m, y, 1, {"inner": z - 1})

    def weight_y(b, m):
        return weight_copy(b, m, y, 2, y_dev)

    goes_up = lambda b: (b <= z) & (z < 3)
    goes_down = lambda b: (b >= z) & (z > 0)

    def pass_on(b, m):
        pl.when(goes_up(b))(lambda: weight_up(b, m).start())
        pl.when(goes_down(b))(lambda: weight_down(b, m).start())

    def arrive(n, m):
        b = order[n]
        weight_copy(b, m, y, 0, y_dev).wait_recv()
        pass_on(b, m)
        weight_y(b, m).start()

    def weight_ready(n):
        for m in range(PIECES):
            weight_copy(order[n], m, 1 - y, 2, y_dev).wait_recv()

    middle = u == 1

    def arrive_early(n, m):
        pl.when(middle)(lambda: arrive(n + 1, m))
        pl.when(jnp.logical_not(middle))(lambda: arrive(n, m))

    def to_flat(d):
        at = pl.ds(pl.multiple_of(d * shard_rows, shard_rows), shard_rows)
        flat[at, :] = slots[d].astype(jnp.float32)[:shard_rows]

    slot_z = [None] + [send(slots.at[own], slots.at[own], z_devs[k]) for k in range(1, 4)]
    slot_x = [send(slots.at[own], slots.at[own], x_dev)]
    slot_core = [send(slots.at[own], slots.at[own], core_dev)]
    for k in range(1, 4):
        slot_z[k].wait_recv()
        at = slots.at[o * 4 + z_from[k]]
        slot_x.append(send(at, at, x_dev))
        slot_core.append(send(at, at, core_dev))
    load_w.wait()
    for m in range(PIECES):
        pass_on(z, m)
    load_up.wait()
    u_x = send(up_all.at[o], up_all.at[o], x_dev)
    u_core = send(up_all.at[o], up_all.at[o], core_dev)
    for k in range(4):
        to_flat(o * 4 + z_from[k])
    for k in range(4):
        slot_x[k].wait_recv()
        at = slots.at[o_x * 4 + z_from[k]]
        slot_core.append(send(at, at, core_dev))
    for k in range(4):
        to_flat(o_x * 4 + z_from[k])
    for k in range(8):
        slot_core[k].wait_recv()
        to_flat((o_core if k < 4 else o_diag) * 4 + z_from[k % 4])

    per_up = value_width // LANES
    up_m = jnp.concatenate(
        [flat[pl.ds(down_rows + j, rank, stride=per_up), :] for j in range(per_up)], axis=1
    ).astype(jnp.bfloat16)
    per_row = width // LANES

    def down_part(first, count):
        rows = [flat[pl.ds(first + j, rank, stride=per_row), :] for j in range(count)]
        return jnp.concatenate(rows, axis=1).astype(jnp.bfloat16)

    own_rank_t = jnp.transpose(dot(up_all[o], up_m, (1, 1))).astype(jnp.bfloat16)
    load_act.wait()

    def part(n, projected):
        cols = pl.ds(pl.multiple_of(n * CHUNK, CHUNK), CHUNK)
        a_part = act_ref[:, cols]
        g_part = scale * dot(own_rank_t, a_part, (1, 0))
        for j in range(CHUNK // LANES):
            at = pl.ds(n * (CHUNK // LANES) + j, rank, stride=per_row)
            grad[at, :] = g_part[:, j * LANES : (j + 1) * LANES]
        return projected + dot(a_part, down_part(n * (CHUNK // LANES), CHUNK // LANES), (1, 1))

    projected = lax.fori_loop(
        0, width // CHUNK, part, jnp.zeros((tokens, rank), jnp.float32)
    ).astype(jnp.bfloat16)
    u_x.wait_recv()
    u_far = send(up_all.at[o_x], up_all.at[o_x], core_dev)
    arrive(1, 0)
    pl.when(middle)(lambda: arrive(2, 0))
    g_up = scale * dot(projected, up_all[o], (0, 0))
    for j in range(per_up):
        grad[pl.ds(down_rows + j, rank, stride=per_up), :] = g_up[:, j * LANES : (j + 1) * LANES]

    part_rows = 2 * shard_rows
    parts = [pl.ds(p * part_rows, part_rows) for p in range(2)]

    def grad_rows(at, p):
        return pl.ds(pl.multiple_of((2 * at + p) * part_rows, part_rows), part_rows)

    g_core_far = [
        send(grad.at[grad_rows(o_diag, p)], from_core.at[0, parts[p]], core_dev) for p in range(2)
    ]
    g_core_own = [
        send(grad.at[grad_rows(o_core, p)], from_core.at[1, parts[p]], core_dev) for p in range(2)
    ]
    u_core.wait_recv()
    u_far.wait_recv()
    u_rows = 4 * tokens
    rank_all = dot(up_all[...].reshape(u_rows, value_width), up_m, (1, 1)).astype(jnp.bfloat16)

    block_copies = []

    def block_cols(n, h):
        at = (o * 4 + order[n]) * 2 + (y if h == 0 else 1 - y)
        return pl.ds(pl.multiple_of(at * half, half), half)

    def block_math(n, h):
        side = y if h == 0 else 1 - y
        per_block = half // LANES
        d_block = down_part(((o * 4 + order[n]) * 2 + side) * per_block, per_block)
        w = w_buf[order[n], pl.ds(pl.multiple_of(side * half, half), half), :]
        value = dot(up_all[...].reshape(u_rows, value_width), w, (1, 1))
        value += scale * dot(rank_all, d_block, (1, 0))
        blocks[n, h] = value.astype(jnp.bfloat16).reshape(4, tokens, half)
        out_ref[:, block_cols(n, h)] = blocks[n, h, o]

    def block_send(n, h):
        for to, device in ((o_x, x_dev), (o_diag, diag_dev), (o_core, core_dev)):
            block_copies.append(
                send(blocks.at[n, h, to], out_ref.at[:, block_cols(n, h)], device)
            )

    def block(n, h):
        block_math(n, h)
        block_send(n, h)

    block(0, 0)
    block(0, 1)
    g_x = []
    for p in range(2):
        g_core_far[p].wait_recv()
        half_sum[0, parts[p]] = grad[grad_rows(o_x, p), :] + from_core[0, parts[p]]
        g_x.append(send(half_sum.at[0, parts[p]], from_x.at[parts[p]], x_dev))
    arrive(1, 1)
    pl.when(middle)(lambda: arrive(2, 1))
    arrive_early(2, 0)
    for p in range(2):
        g_core_own[p].wait_recv()
        half_sum[1, parts[p]] = grad[grad_rows(o, p), :] + from_core[1, parts[p]]
    arrive_early(2, 1)
    block_math(1, 0)
    weight_ready(1)
    block_math(1, 1)

    def shard(at):
        return pl.ds(pl.multiple_of(at * shard_rows, shard_rows), shard_rows)

    def shard_copy(to, source):
        return pltpu.make_async_remote_copy(
            src_ref=half_sum.at[1, shard(to)],
            dst_ref=from_z.at[source],
            send_sem=shard_send_sem.at[to],
            recv_sem=shard_recv_sem.at[source],
            device_id={"inner": to},
            device_id_type=MESH,
        )

    for p in range(2):
        g_x[p].wait_recv()
        half_sum[1, parts[p]] += from_x[parts[p]]
        for to in (2 * p, 2 * p + 1):
            pl.when(z != to)(lambda to=to: shard_copy(to, z).start())
        if p == 0:
            pl.when(jnp.logical_not(middle))(lambda: arrive(3, 0))
    block_send(1, 0)
    block_send(1, 1)
    pl.when(jnp.logical_not(middle))(lambda: arrive(3, 1))
    block(2, 0)
    weight_ready(2)
    block(2, 1)
    block(3, 0)
    for k in range(1, 4):
        shard_copy(z_to[k], z_from[k]).wait_recv()
    total = half_sum[1, shard(z), :]
    for k in range(1, 4):
        total += from_z[z_from[k]]
    clipped_ref[...] = total
    sq_own[...] = jnp.sum((total * total).reshape(shard_rows // 8, 8, LANES), axis=0)
    s_z = [send(sq_own, sq_z.at[k - 1], z_devs[k]) for k in range(1, 4)]
    weight_ready(3)
    block(3, 1)
    for copy in s_z:
        copy.wait_recv()
    sq_line[...] = sq_own[...] + sq_z[0] + sq_z[1] + sq_z[2]
    s_s = [
        send(sq_line, sq_s.at[n], device)
        for n, device in enumerate((core_dev, x_dev, diag_dev))
    ]
    for copy in s_s:
        copy.wait_recv()
    sum_squares = jnp.sum(sq_line[...] + sq_s[0] + sq_s[1] + sq_s[2], keepdims=True)
    norm = jnp.sqrt(sum_squares + 1e-06)
    clipped_ref[...] = clipped_ref[...] * jnp.minimum(1.0, math.sqrt(params) / norm)
    for copy in block_copies:
        copy.wait_recv()
    for copy in used:
        copy.wait_send()
    for k in range(1, 4):
        shard_copy(z_to[k], z).wait_send()
    for n in range(4):
        for m in range(PIECES):
            b = order[n]
            pl.when(goes_up(b))(lambda b=b, m=m: weight_up(b, m).wait_send())
            pl.when(goes_down(b))(lambda b=b, m=m: weight_down(b, m).wait_send())
            if n > 0:
                weight_y(b, m).wait_send()


def finish(rows_in, *refs):
    states_in, rows_out, states_out = refs[:4], refs[4], refs[5:8]
    held, held_in, held_out, in_sem, out_sem = refs[8:]
    step = rows_in.shape[0] // ROW_COPIES
    cuts = [pl.ds(n * step, step) for n in range(ROW_COPIES)]
    moves = [(rows_in.at[at], held.at[at]) for at in cuts]
    moves += [(ref, held_in.at[n]) for n, ref in enumerate(states_in)]
    fetch = [pltpu.make_async_copy(a, b, in_sem.at[n]) for n, (a, b) in enumerate(moves)]
    moves = [(held.at[at], rows_out.at[at]) for at in cuts]
    moves += [(held_out.at[n], ref) for n, ref in enumerate(states_out)]
    put = [pltpu.make_async_copy(a, b, out_sem.at[n]) for n, (a, b) in enumerate(moves)]
    for copy in fetch:
        copy.start()
    for n in range(ROW_COPIES):
        fetch[n].wait()
        put[n].start()
    for copy in fetch[ROW_COPIES:]:
        copy.wait()
    held_out[0], held_out[1], held_out[2] = adam(*(held_in[n] for n in range(4)))
    for copy in put[ROW_COPIES:]:
        copy.start()
    for copy in put:
        copy.wait()


N_COPIES = 64


def fused(rank, activations, upstream, weight, master, moment, second_moment):
    tokens, width = activations.shape
    value_width = upstream.shape[1]
    feats = weight.shape[0]
    shard_rows = master.shape[0] // LANES
    flat_rows = 16 * shard_rows
    padded = -(-shard_rows // 16) * 16
    state = jax.ShapeDtypeStruct((shard_rows, LANES), jnp.float32)
    bf16, f32 = jnp.bfloat16, jnp.float32
    vmem = pl.BlockSpec(memory_space=pltpu.VMEM)
    hbm = pl.BlockSpec(memory_space=pltpu.HBM)
    rows, clipped = pl.pallas_call(
        functools.partial(kernel, rank),
        out_shape=(jax.ShapeDtypeStruct((tokens, width), bf16), state),
        in_specs=[hbm] * 4,
        out_specs=(vmem,) * 2,
        scratch_shapes=[
            pltpu.VMEM((tokens, width), bf16),
            pltpu.VMEM((shard_rows, LANES), f32),
            pltpu.VMEM((16, padded, LANES), bf16),
            pltpu.VMEM((flat_rows, LANES), f32),
            pltpu.VMEM((4, tokens, value_width), bf16),
            pltpu.VMEM((4, feats, value_width), bf16),
            pltpu.VMEM((flat_rows, LANES), f32),
            pltpu.VMEM((2, 4 * shard_rows, LANES), f32),
            pltpu.VMEM((2, 4 * shard_rows, LANES), f32),
            pltpu.VMEM((4 * shard_rows, LANES), f32),
            pltpu.VMEM((4, shard_rows, LANES), f32),
            pltpu.VMEM((8, LANES), f32),
            pltpu.VMEM((3, 8, LANES), f32),
            pltpu.VMEM((8, LANES), f32),
            pltpu.VMEM((3, 8, LANES), f32),
            pltpu.VMEM((4, 2, 4, tokens, feats // 2), bf16),
            pltpu.SemaphoreType.DMA((4,)),
            pltpu.SemaphoreType.DMA((N_COPIES,)),
            pltpu.SemaphoreType.DMA((N_COPIES,)),
            pltpu.SemaphoreType.DMA((3, PIECES, 4)),
            pltpu.SemaphoreType.DMA((2, PIECES, 4)),
            pltpu.SemaphoreType.DMA((4,)),
            pltpu.SemaphoreType.DMA((4,)),
        ],
        compiler_params=pltpu.CompilerParams(
            collective_id=0, has_side_effects=True, vmem_limit_bytes=VMEM_GRANT
        ),
        name="adapter_backward",
    )(activations, upstream, weight, master.reshape(shard_rows, LANES))
    result = pl.pallas_call(
        finish,
        out_shape=(jax.ShapeDtypeStruct((tokens, width), bf16), state, state, state),
        in_specs=[hbm] * 5,
        out_specs=(hbm,) * 4,
        scratch_shapes=[
            pltpu.VMEM((tokens, width), bf16),
            pltpu.VMEM((4, shard_rows, LANES), f32),
            pltpu.VMEM((3, shard_rows, LANES), f32),
            pltpu.SemaphoreType.DMA((ROW_COPIES + 4,)),
            pltpu.SemaphoreType.DMA((ROW_COPIES + 3,)),
        ],
        compiler_params=pltpu.CompilerParams(vmem_limit_bytes=VMEM_GRANT),
        name="finish",
    )(
        rows,
        clipped,
        master.reshape(shard_rows, LANES),
        moment.reshape(shard_rows, LANES),
        second_moment.reshape(shard_rows, LANES),
    )
    return (result[0],) + tuple(r.reshape(-1) for r in result[1:])


def solution(mesh):
    sizes = dict(mesh.shape)
    square = sizes["groups"] == 2 and sizes["outer"] == 4 and sizes["inner"] == 4

    def body(activations, upstream, weight, master, moment, second_moment):
        width, value_width = activations.shape[1], upstream.shape[1]
        rank = master.shape[0] * sizes["outer"] * sizes["inner"] // (width + value_width)
        fits = (
            activations.shape[0] % (16 * ROW_COPIES) == 0
            and width % CHUNK == 0
            and value_width % LANES == 0
            and weight.shape[0] % 256 == 0
            and master.shape[0] % (8 * LANES) == 0
            and rank % 16 == 0
        )
        if square and fits:
            return fused(rank, activations, upstream, weight, master, moment, second_moment)
        return per_device(activations, upstream, weight, master, moment, second_moment)

    return jax.shard_map(
        body,
        mesh=mesh,
        in_specs=(
            P(("groups", "outer", "inner"), None),
            P(("groups", "outer", "inner"), None),
            P(("outer", "inner"), None),
            P(("groups", "outer", "inner")),
            P(("groups", "outer", "inner")),
            P(("groups", "outer", "inner")),
        ),
        out_specs=(
            P(("groups", "outer", "inner"), None),
            P(("groups", "outer", "inner")),
            P(("groups", "outer", "inner")),
            P(("groups", "outer", "inner")),
        ),
        check_vma=False,
    )
```

```python
import functools
import math

import jax
import jax.numpy as jnp
from jax import lax
from jax.experimental import pallas as pl
from jax.experimental.pallas import tpu as pltpu
from jax.sharding import PartitionSpec as P

MESH = pl.DeviceIdType.MESH
LANES = 128
CHUNK = 1024
PIECES = 2
ROW_COPIES = 4
VMEM_GRANT = 56 * 1024 * 1024


def per_device(activations, upstream, frozen_weight_matrix, master, moment, second_moment):
    width = activations.shape[1]
    value_width = upstream.shape[1]
    whole = lax.all_gather(master.astype(jnp.bfloat16), ("outer", "inner"), axis=0, tiled=True)
    rank_activations = whole.shape[0] // (width + value_width)
    adapter_scale_factor = 0.5 / math.sqrt(rank_activations * value_width)
    down_weight_transposed = whole[: rank_activations * width].reshape(rank_activations, width)
    up_m = whole[rank_activations * width :].reshape(rank_activations, value_width)
    rank_gradient = jnp.dot(upstream, up_m.T, preferred_element_type=jnp.float32).astype(
        jnp.bfloat16
    )
    projected_rows = jnp.dot(
        activations, down_weight_transposed.T, preferred_element_type=jnp.float32
    ).astype(jnp.bfloat16)
    down_weight_gradient = adapter_scale_factor * jnp.dot(
        rank_gradient.T, activations, preferred_element_type=jnp.float32
    )
    up_weight_gradient = adapter_scale_factor * jnp.dot(
        projected_rows.T, upstream, preferred_element_type=jnp.float32
    )
    flat_grad = jnp.concatenate([down_weight_gradient.reshape(-1), up_weight_gradient.reshape(-1)])
    grad_shard = lax.psum_scatter(flat_grad, ("outer", "inner"), scatter_dimension=0, tiled=True)
    sum_squares = lax.psum(jnp.sum(grad_shard * grad_shard), ("outer", "inner"))
    feat_rows = frozen_weight_matrix.shape[0]
    feat_start = lax.axis_index(("outer", "inner")) * feat_rows
    own_cols = lax.dynamic_slice_in_dim(down_weight_transposed, feat_start, feat_rows, 1)
    tok_piece = lax.all_gather(upstream, ("outer", "inner"), axis=0, tiled=True)
    rank_piece = jnp.dot(tok_piece, up_m.T, preferred_element_type=jnp.float32).astype(jnp.bfloat16)
    frozen_output = lax.dot_general(
        tok_piece,
        frozen_weight_matrix,
        (((1,), (1,)), ((), ())),
        preferred_element_type=jnp.float32,
    )
    feat_block = (
        frozen_output
        + adapter_scale_factor * jnp.dot(rank_piece, own_cols, preferred_element_type=jnp.float32)
    ).astype(jnp.bfloat16)
    n_outer = lax.axis_size("outer")
    n_inner = lax.axis_size("inner")
    tok_count = upstream.shape[0]
    reordered = (
        feat_block.reshape(n_outer, n_inner, tok_count, feat_rows)
        .transpose(1, 0, 2, 3)
        .reshape(n_inner * n_outer * tok_count, feat_rows)
    )
    input_gradient_rows = lax.all_to_all(
        lax.all_to_all(reordered, "inner", split_axis=0, concat_axis=1, tiled=True),
        "outer",
        split_axis=0,
        concat_axis=1,
        tiled=True,
    )
    norm = jnp.sqrt(sum_squares + 1e-06)
    clipped = grad_shard * jnp.minimum(1.0, math.sqrt(whole.shape[0]) / norm)
    return (input_gradient_rows,) + adam(clipped, master, moment, second_moment)


def adam(clipped, master, moment, second_moment):
    new_moment = 0.9 * moment + 0.1 * clipped
    new_second = 0.999 * second_moment + 0.001 * clipped * clipped
    corr_one = 1.0 - 0.9**10
    corr_two = 1.0 - 0.999**10
    new_master = master - 0.1 * (new_moment / corr_one) / (jnp.sqrt(new_second / corr_two) + 1e-08)
    return new_master, new_moment, new_second


def dot(a, b, contract):
    return lax.dot_general(
        a, b, (((contract[0],), (contract[1],)), ((), ())), preferred_element_type=jnp.float32
    )


def kernel(
    rank,
    act_hbm,
    up_hbm,
    w_hbm,
    master_hbm,
    out_ref,
    clipped_ref,
    act_ref,
    master_ref,
    slots,
    flat,
    up_all,
    w_buf,
    grad,
    from_core,
    half_sum,
    from_x,
    from_z,
    sq_own,
    sq_z,
    sq_line,
    sq_s,
    blocks,
    load_sem,
    send_sem,
    recv_sem,
    w_send_sem,
    w_recv_sem,
    shard_send_sem,
    shard_recv_sem,
):
    y = lax.axis_index("groups")
    o = lax.axis_index("outer")
    z = lax.axis_index("inner")
    x, c = o // 2, lax.rem(o, 2)
    o_core = 2 * x + (1 - c)
    o_x = 2 * (1 - x) + c
    o_diag = 2 * (1 - x) + (1 - c)
    core_dev, x_dev, diag_dev = {"outer": o_core}, {"outer": o_x}, {"outer": o_diag}
    y_dev = {"groups": 1 - y}
    z_to = [None] + [lax.rem(z + k, 4) for k in range(1, 4)]
    z_from = [z] + [lax.rem(z + 4 - k, 4) for k in range(1, 4)]
    z_devs = [None] + [{"inner": z_to[k]} for k in range(1, 4)]
    high = z // 2
    u = z + high * (3 - 2 * z)
    order = [z] + [f + high * (3 - 2 * f) for f in (1 - u, 2, 3)]

    tokens, width = act_ref.shape
    value_width = up_all.shape[2]
    feats = w_buf.shape[1]
    half = feats // 2
    shard_rows = master_ref.shape[0]
    down_rows = rank * width // LANES
    params = 16 * shard_rows * LANES
    scale = 0.5 / math.sqrt(rank * value_width)

    barrier = pltpu.get_barrier_semaphore()
    partners = [core_dev, x_dev, diag_dev, y_dev] + z_devs[1:]
    for device in partners:
        pl.semaphore_signal(barrier, inc=1, device_id=device, device_id_type=MESH)

    loads = [
        pltpu.make_async_copy(src, dst, load_sem.at[n])
        for n, (src, dst) in enumerate(
            (
                (master_hbm, master_ref),
                (up_hbm, up_all.at[o]),
                (w_hbm, w_buf.at[z]),
                (act_hbm, act_ref),
            )
        )
    ]
    for load in loads:
        load.start()
    load_master, load_up, load_w, load_act = loads

    used = []

    def send(src, dst, device):
        at = len(used)
        copy = pltpu.make_async_remote_copy(
            src_ref=src,
            dst_ref=dst,
            send_sem=send_sem.at[at],
            recv_sem=recv_sem.at[at],
            device_id=device,
            device_id_type=MESH,
        )
        used.append(copy)
        copy.start()
        return copy

    own = o * 4 + z
    pad = slots.shape[1] - shard_rows
    load_master.wait()
    slots[own] = jnp.concatenate(
        [master_ref[...], jnp.zeros((pad, LANES), jnp.float32)], axis=0
    ).astype(jnp.bfloat16)
    pl.semaphore_wait(barrier, len(partners))

    piece = half // PIECES

    def weight_rows(part_y, m):
        return pl.ds(pl.multiple_of(part_y * half + m * piece, piece), piece)

    def weight_copy(b, m, part_y, way, device):
        at = w_buf.at[b, weight_rows(part_y, m)]
        return pltpu.make_async_remote_copy(
            src_ref=at,
            dst_ref=at,
            send_sem=w_send_sem.at[way, m, b],
            recv_sem=w_recv_sem.at[way // 2, m, b],
            device_id=device,
            device_id_type=MESH,
        )

    def weight_up(b, m):
        return weight_copy(b, m, y, 0, {"inner": z + 1})

    def weight_down(b, m):
        return weight_copy(b, m, y, 1, {"inner": z - 1})

    def weight_y(b, m):
        return weight_copy(b, m, y, 2, y_dev)

    goes_up = lambda b: (b <= z) & (z < 3)
    goes_down = lambda b: (b >= z) & (z > 0)

    def pass_on(b, m):
        pl.when(goes_up(b))(lambda: weight_up(b, m).start())
        pl.when(goes_down(b))(lambda: weight_down(b, m).start())

    def arrive(n, m):
        b = order[n]
        weight_copy(b, m, y, 0, y_dev).wait_recv()
        pass_on(b, m)
        weight_y(b, m).start()

    def weight_ready(n):
        for m in range(PIECES):
            weight_copy(order[n], m, 1 - y, 2, y_dev).wait_recv()

    middle = u == 1

    def arrive_early(n, m):
        pl.when(middle)(lambda: arrive(n + 1, m))
        pl.when(jnp.logical_not(middle))(lambda: arrive(n, m))

    def to_flat(d):
        at = pl.ds(pl.multiple_of(d * shard_rows, shard_rows), shard_rows)
        flat[at, :] = slots[d].astype(jnp.float32)[:shard_rows]

    slot_z = [None] + [send(slots.at[own], slots.at[own], z_devs[k]) for k in range(1, 4)]
    slot_x = [send(slots.at[own], slots.at[own], x_dev)]
    slot_core = [send(slots.at[own], slots.at[own], core_dev)]
    load_up.wait()
    u_x = send(up_all.at[o], up_all.at[o], x_dev)
    u_core = send(up_all.at[o], up_all.at[o], core_dev)
    load_w.wait()
    pass_on(z, 0)
    for k in range(1, 4):
        slot_z[k].wait_recv()
        at = slots.at[o * 4 + z_from[k]]
        slot_x.append(send(at, at, x_dev))
        slot_core.append(send(at, at, core_dev))
    for m in range(1, PIECES):
        pass_on(z, m)
    for k in range(4):
        to_flat(o * 4 + z_from[k])
    for k in range(4):
        slot_x[k].wait_recv()
        at = slots.at[o_x * 4 + z_from[k]]
        slot_core.append(send(at, at, core_dev))
    u_x.wait_recv()
    u_far = send(up_all.at[o_x], up_all.at[o_x], core_dev)
    for k in range(4):
        to_flat(o_x * 4 + z_from[k])
    for k in range(8):
        slot_core[k].wait_recv()
        to_flat((o_core if k < 4 else o_diag) * 4 + z_from[k % 4])

    per_up = value_width // LANES
    up_m = jnp.concatenate(
        [flat[pl.ds(down_rows + j, rank, stride=per_up), :] for j in range(per_up)], axis=1
    ).astype(jnp.bfloat16)
    per_row = width // LANES

    def down_part(first, count):
        rows = [flat[pl.ds(first + j, rank, stride=per_row), :] for j in range(count)]
        return jnp.concatenate(rows, axis=1).astype(jnp.bfloat16)

    u_core.wait_recv()
    u_far.wait_recv()
    u_rows = 4 * tokens
    rank_all = dot(up_all[...].reshape(u_rows, value_width), up_m, (1, 1)).astype(jnp.bfloat16)

    block_copies = []

    def block_cols(n, h):
        at = (o * 4 + order[n]) * 2 + (y if h == 0 else 1 - y)
        return pl.ds(pl.multiple_of(at * half, half), half)

    def block_math(n, h):
        side = y if h == 0 else 1 - y
        per_block = half // LANES
        d_block = down_part(((o * 4 + order[n]) * 2 + side) * per_block, per_block)
        w = w_buf[order[n], pl.ds(pl.multiple_of(side * half, half), half), :]
        value = dot(up_all[...].reshape(u_rows, value_width), w, (1, 1))
        value += scale * dot(rank_all, d_block, (1, 0))
        blocks[n, h] = value.astype(jnp.bfloat16).reshape(4, tokens, half)
        out_ref[:, block_cols(n, h)] = blocks[n, h, o]

    def block_send(n, h):
        for to, device in ((o_x, x_dev), (o_diag, diag_dev), (o_core, core_dev)):
            block_copies.append(
                send(blocks.at[n, h, to], out_ref.at[:, block_cols(n, h)], device)
            )

    def block(n, h):
        block_math(n, h)
        block_send(n, h)

    arrive(1, 0)
    pl.when(middle)(lambda: arrive(2, 0))
    block(0, 0)
    block(0, 1)
    arrive(1, 1)
    pl.when(middle)(lambda: arrive(2, 1))

    own_rank_t = jnp.transpose(dot(up_all[o], up_m, (1, 1))).astype(jnp.bfloat16)
    load_act.wait()

    def part(n, projected):
        cols = pl.ds(pl.multiple_of(n * CHUNK, CHUNK), CHUNK)
        a_part = act_ref[:, cols]
        g_part = scale * dot(own_rank_t, a_part, (1, 0))
        for j in range(CHUNK // LANES):
            at = pl.ds(n * (CHUNK // LANES) + j, rank, stride=per_row)
            grad[at, :] = g_part[:, j * LANES : (j + 1) * LANES]
        return projected + dot(a_part, down_part(n * (CHUNK // LANES), CHUNK // LANES), (1, 1))

    projected = lax.fori_loop(
        0, width // CHUNK, part, jnp.zeros((tokens, rank), jnp.float32)
    ).astype(jnp.bfloat16)
    g_up = scale * dot(projected, up_all[o], (0, 0))
    for j in range(per_up):
        grad[pl.ds(down_rows + j, rank, stride=per_up), :] = g_up[:, j * LANES : (j + 1) * LANES]

    part_rows = 2 * shard_rows
    parts = [pl.ds(p * part_rows, part_rows) for p in range(2)]

    def grad_rows(at, p):
        return pl.ds(pl.multiple_of((2 * at + p) * part_rows, part_rows), part_rows)

    g_core_far = [
        send(grad.at[grad_rows(o_diag, p)], from_core.at[0, parts[p]], core_dev) for p in range(2)
    ]
    g_core_own = [
        send(grad.at[grad_rows(o_core, p)], from_core.at[1, parts[p]], core_dev) for p in range(2)
    ]
    arrive_early(2, 0)
    g_x = []
    for p in range(2):
        g_core_far[p].wait_recv()
        half_sum[0, parts[p]] = grad[grad_rows(o_x, p), :] + from_core[0, parts[p]]
        g_x.append(send(half_sum.at[0, parts[p]], from_x.at[parts[p]], x_dev))
    for p in range(2):
        g_core_own[p].wait_recv()
        half_sum[1, parts[p]] = grad[grad_rows(o, p), :] + from_core[1, parts[p]]
    arrive_early(2, 1)
    block_math(1, 0)
    weight_ready(1)
    block_math(1, 1)

    def shard(at):
        return pl.ds(pl.multiple_of(at * shard_rows, shard_rows), shard_rows)

    def shard_copy(to, source):
        return pltpu.make_async_remote_copy(
            src_ref=half_sum.at[1, shard(to)],
            dst_ref=from_z.at[source],
            send_sem=shard_send_sem.at[to],
            recv_sem=shard_recv_sem.at[source],
            device_id={"inner": to},
            device_id_type=MESH,
        )

    for p in range(2):
        g_x[p].wait_recv()
        half_sum[1, parts[p]] += from_x[parts[p]]
        for to in (2 * p, 2 * p + 1):
            pl.when(z != to)(lambda to=to: shard_copy(to, z).start())
        if p == 0:
            pl.when(jnp.logical_not(middle))(lambda: arrive(3, 0))
    block_send(1, 0)
    block_send(1, 1)
    pl.when(jnp.logical_not(middle))(lambda: arrive(3, 1))
    block(2, 0)
    weight_ready(2)
    block(2, 1)
    block(3, 0)
    for k in range(1, 4):
        shard_copy(z_to[k], z_from[k]).wait_recv()
    total = half_sum[1, shard(z), :]
    for k in range(1, 4):
        total += from_z[z_from[k]]
    clipped_ref[...] = total
    sq_own[...] = jnp.sum((total * total).reshape(shard_rows // 8, 8, LANES), axis=0)
    s_z = [send(sq_own, sq_z.at[k - 1], z_devs[k]) for k in range(1, 4)]
    weight_ready(3)
    block(3, 1)
    for copy in s_z:
        copy.wait_recv()
    sq_line[...] = sq_own[...] + sq_z[0] + sq_z[1] + sq_z[2]
    s_s = [
        send(sq_line, sq_s.at[n], device)
        for n, device in enumerate((core_dev, x_dev, diag_dev))
    ]
    for copy in s_s:
        copy.wait_recv()
    sum_squares = jnp.sum(sq_line[...] + sq_s[0] + sq_s[1] + sq_s[2], keepdims=True)
    norm = jnp.sqrt(sum_squares + 1e-06)
    clipped_ref[...] = clipped_ref[...] * jnp.minimum(1.0, math.sqrt(params) / norm)
    for copy in block_copies:
        copy.wait_recv()
    for copy in used:
        copy.wait_send()
    for k in range(1, 4):
        shard_copy(z_to[k], z).wait_send()
    for n in range(4):
        for m in range(PIECES):
            b = order[n]
            pl.when(goes_up(b))(lambda b=b, m=m: weight_up(b, m).wait_send())
            pl.when(goes_down(b))(lambda b=b, m=m: weight_down(b, m).wait_send())
            if n > 0:
                weight_y(b, m).wait_send()


def finish(rows_in, *refs):
    states_in, rows_out, states_out = refs[:4], refs[4], refs[5:8]
    held, held_in, held_out, in_sem, out_sem = refs[8:]
    step = rows_in.shape[0] // ROW_COPIES
    cuts = [pl.ds(n * step, step) for n in range(ROW_COPIES)]
    moves = [(rows_in.at[at], held.at[at]) for at in cuts]
    moves += [(ref, held_in.at[n]) for n, ref in enumerate(states_in)]
    fetch = [pltpu.make_async_copy(a, b, in_sem.at[n]) for n, (a, b) in enumerate(moves)]
    moves = [(held.at[at], rows_out.at[at]) for at in cuts]
    moves += [(held_out.at[n], ref) for n, ref in enumerate(states_out)]
    put = [pltpu.make_async_copy(a, b, out_sem.at[n]) for n, (a, b) in enumerate(moves)]
    for copy in fetch:
        copy.start()
    for n in range(ROW_COPIES):
        fetch[n].wait()
        put[n].start()
    for copy in fetch[ROW_COPIES:]:
        copy.wait()
    held_out[0], held_out[1], held_out[2] = adam(*(held_in[n] for n in range(4)))
    for copy in put[ROW_COPIES:]:
        copy.start()
    for copy in put:
        copy.wait()


N_COPIES = 64


def fused(rank, activations, upstream, weight, master, moment, second_moment):
    tokens, width = activations.shape
    value_width = upstream.shape[1]
    feats = weight.shape[0]
    shard_rows = master.shape[0] // LANES
    flat_rows = 16 * shard_rows
    padded = -(-shard_rows // 16) * 16
    state = jax.ShapeDtypeStruct((shard_rows, LANES), jnp.float32)
    bf16, f32 = jnp.bfloat16, jnp.float32
    vmem = pl.BlockSpec(memory_space=pltpu.VMEM)
    hbm = pl.BlockSpec(memory_space=pltpu.HBM)
    rows, clipped = pl.pallas_call(
        functools.partial(kernel, rank),
        out_shape=(jax.ShapeDtypeStruct((tokens, width), bf16), state),
        in_specs=[hbm] * 4,
        out_specs=(vmem,) * 2,
        scratch_shapes=[
            pltpu.VMEM((tokens, width), bf16),
            pltpu.VMEM((shard_rows, LANES), f32),
            pltpu.VMEM((16, padded, LANES), bf16),
            pltpu.VMEM((flat_rows, LANES), f32),
            pltpu.VMEM((4, tokens, value_width), bf16),
            pltpu.VMEM((4, feats, value_width), bf16),
            pltpu.VMEM((flat_rows, LANES), f32),
            pltpu.VMEM((2, 4 * shard_rows, LANES), f32),
            pltpu.VMEM((2, 4 * shard_rows, LANES), f32),
            pltpu.VMEM((4 * shard_rows, LANES), f32),
            pltpu.VMEM((4, shard_rows, LANES), f32),
            pltpu.VMEM((8, LANES), f32),
            pltpu.VMEM((3, 8, LANES), f32),
            pltpu.VMEM((8, LANES), f32),
            pltpu.VMEM((3, 8, LANES), f32),
            pltpu.VMEM((4, 2, 4, tokens, feats // 2), bf16),
            pltpu.SemaphoreType.DMA((4,)),
            pltpu.SemaphoreType.DMA((N_COPIES,)),
            pltpu.SemaphoreType.DMA((N_COPIES,)),
            pltpu.SemaphoreType.DMA((3, PIECES, 4)),
            pltpu.SemaphoreType.DMA((2, PIECES, 4)),
            pltpu.SemaphoreType.DMA((4,)),
            pltpu.SemaphoreType.DMA((4,)),
        ],
        compiler_params=pltpu.CompilerParams(
            collective_id=0, has_side_effects=True, vmem_limit_bytes=VMEM_GRANT
        ),
        name="adapter_backward",
    )(activations, upstream, weight, master.reshape(shard_rows, LANES))
    result = pl.pallas_call(
        finish,
        out_shape=(jax.ShapeDtypeStruct((tokens, width), bf16), state, state, state),
        in_specs=[hbm] * 5,
        out_specs=(hbm,) * 4,
        scratch_shapes=[
            pltpu.VMEM((tokens, width), bf16),
            pltpu.VMEM((4, shard_rows, LANES), f32),
            pltpu.VMEM((3, shard_rows, LANES), f32),
            pltpu.SemaphoreType.DMA((ROW_COPIES + 4,)),
            pltpu.SemaphoreType.DMA((ROW_COPIES + 3,)),
        ],
        compiler_params=pltpu.CompilerParams(vmem_limit_bytes=VMEM_GRANT),
        name="finish",
    )(
        rows,
        clipped,
        master.reshape(shard_rows, LANES),
        moment.reshape(shard_rows, LANES),
        second_moment.reshape(shard_rows, LANES),
    )
    return (result[0],) + tuple(r.reshape(-1) for r in result[1:])


def solution(mesh):
    sizes = dict(mesh.shape)
    square = sizes["groups"] == 2 and sizes["outer"] == 4 and sizes["inner"] == 4

    def body(activations, upstream, weight, master, moment, second_moment):
        width, value_width = activations.shape[1], upstream.shape[1]
        rank = master.shape[0] * sizes["outer"] * sizes["inner"] // (width + value_width)
        fits = (
            activations.shape[0] % (16 * ROW_COPIES) == 0
            and width % CHUNK == 0
            and value_width % LANES == 0
            and weight.shape[0] % 256 == 0
            and master.shape[0] % (8 * LANES) == 0
            and rank % 16 == 0
        )
        if square and fits:
            return fused(rank, activations, upstream, weight, master, moment, second_moment)
        return per_device(activations, upstream, weight, master, moment, second_moment)

    return jax.shard_map(
        body,
        mesh=mesh,
        in_specs=(
            P(("groups", "outer", "inner"), None),
            P(("groups", "outer", "inner"), None),
            P(("outer", "inner"), None),
            P(("groups", "outer", "inner")),
            P(("groups", "outer", "inner")),
            P(("groups", "outer", "inner")),
        ),
        out_specs=(
            P(("groups", "outer", "inner"), None),
            P(("groups", "outer", "inner")),
            P(("groups", "outer", "inner")),
            P(("groups", "outer", "inner")),
        ),
        check_vma=False,
    )
```
